32 devices in a mesh: rep: 4 (over y, x), fsdp: 8 (over z, core).
Axes of the slice: x: 2, y: 2, z: 4, core: 2. Of those that a mesh axis runs over, the one named last changes fastest.
Arguments:
- grad_blocks: bfloat16 [4, 8, 512, 512], P('rep', None, 'fsdp'), may hold values from -6 to 6
- graft_accum: float32 [8, 512, 512], P(None, 'fsdp'), may hold values from 0.1 to 1000000
- left_stats: float32 [16, 512, 512], P('fsdp'), may hold values from -300000 to 300000, as said below
- right_stats: float32 [16, 512, 512], P('fsdp'), may hold values from -300000 to 300000, as said below
- block_slot: int32 [8], replicated, may hold values from 0 to 15, as said below
- vocab_grads: bfloat16 [4, 2, 64, 8192], P('rep', None, 'fsdp'), may hold values from -6 to 6
- vocab_accum: float32 [2, 64, 8192], P(None, 'fsdp'), may hold values from 0.01 to 10
Outputs:
- direction: bfloat16 [8, 512, 512], P(None, 'fsdp')
- graft_accum_new: float32 [8, 512, 512], P(None, 'fsdp')
- left_new: float32 [16, 512, 512], P('fsdp')
- right_new: float32 [16, 512, 512], P('fsdp')
- vocab_accum_new: float32 [2, 64, 8192], P(None, 'fsdp')
- vocab_step: bfloat16 [2, 64, 8192], P(None, 'fsdp')
The draws below stay inside these ranges and needn't reach their ends.
Inputs may be any that keep to these rules, and one draw needn't show every extreme that they name: Block b's statistics sit in slot block_slot[b]; slot s belongs to fsdp index s // 2; no two blocks name the same slot; every fsdp index owns at most 2 blocks and some index owns exactly 2. `left_stats`: every slot holds a symmetric positive definite matrix. `right_stats`: every slot holds a symmetric positive definite matrix.
All inputs are finite; a program needn't handle non-finite values.
Results may differ from the reference program's by a relative error of at most 0.017.
Values may be sent and summed in bfloat16 or wider, within the bound.
No kernel may reach another device: no remote copies, remote signals or barrier semaphores. Data moves between devices by JAX's collectives and lax.ppermute only.
A program may use at most 64 MiB of HBM per device.

```python
import math
import jax
import jax.numpy as jnp
from jax import lax

D = 8192
B = 512
MOST = 2
ITERS = 6
NBLK = 8
SLOTS = 16
VOC = 64
N_REP = 4


def draw_block_slot(key, part):
    base = jax.random.fold_in(key, 11)
    first_key, second_key, third_key = jax.random.split(base, 3)
    workers = SLOTS // MOST
    full_worker = jax.random.randint(first_key, (), 0, workers)
    shuffled = jax.random.permutation(second_key, SLOTS).astype(jnp.int32)
    priority = (shuffled // MOST != full_worker).astype(jnp.int32) * SLOTS + jnp.arange(SLOTS, dtype=jnp.int32)
    ordered = shuffled[jnp.argsort(priority)]
    chosen = ordered[:NBLK]
    return chosen[jax.random.permutation(third_key, NBLK)].astype(jnp.int32)


def stats_draw(key, salt):
    base = jax.random.fold_in(key, salt)
    slot_keys = jax.random.split(base, SLOTS)
    order = float(B)

    def single(slot_key):
        first_key = jax.random.fold_in(slot_key, 0)
        second_key = jax.random.fold_in(slot_key, 1)
        fourth_key = jax.random.fold_in(slot_key, 3)
        fifth_key = jax.random.fold_in(slot_key, 4)
        factors = jax.random.normal(first_key, (B, 2 * B), jnp.float32)
        gram = jnp.dot(factors, factors.T, precision=lax.Precision.HIGHEST) / (2.0 * order)
        gram = 0.5 * (gram + gram.T)
        wishart_weight = 4.0 * order * jnp.exp(jax.random.uniform(second_key, (), jnp.float32, 0.0, jnp.log(3.0)))
        power = 1.0
        ranks = jax.random.permutation(fourth_key, B).astype(jnp.float32) + 1.0
        top_level = 8.0 * order * math.sqrt(order) * jnp.exp(jax.random.uniform(fifth_key, (), jnp.float32, 0.0, jnp.log(2.0)))
        spikes = top_level * jnp.power(ranks, -power)
        return wishart_weight * gram + jnp.diag(spikes)
    return lax.map(single, slot_keys)


def draw_left_stats(key, part):
    return stats_draw(key, 31)


def draw_right_stats(key, part):
    return stats_draw(key, 37)


def draw_graft_accum(key, part):
    base = jax.random.fold_in(key, 23)
    first_key, second_key, third_key = jax.random.split(base, 3)
    position = (jnp.arange(B, dtype=jnp.float32) / B)[None, :, None]
    jitter = jax.random.uniform(first_key, (NBLK, B, 1), jnp.float32)
    row_power = 2.0 * position + jitter
    column_power = 2.0 * jax.random.uniform(second_key, (NBLK, 1, B), jnp.float32)
    roughness = jax.random.uniform(third_key, (NBLK, B, B), jnp.float32, -0.7, 0.7)
    return jnp.power(10.0, row_power + column_power) * jnp.exp(roughness)


def block_scale(key, extent, cuts, low, high):
    loudness = 1.0
    for dim, blocks in cuts:
        steps = jax.random.uniform(jax.random.fold_in(jax.random.fold_in(key, 6), dim), (blocks,), jnp.float32, low / len(cuts), high / len(cuts))
        loudness = loudness * jnp.repeat(jnp.exp(steps), extent[dim] // blocks).reshape((-1,) + (1,) * (len(extent) - 1 - dim))
    return loudness


def gaussian(rng, shape, scale, limit, cuts=(), kind=jnp.bfloat16):
    loudness = block_scale(rng, shape, cuts, -0.22, 0.18) if cuts else 1.0
    array = jax.random.normal(rng, shape, jnp.float32) * scale * loudness
    return jnp.minimum(jnp.maximum(array, -limit), limit).astype(kind)


def setup_inputs(seed: int = 0) -> dict:
    key_list = jax.random.split(jax.random.key(seed), 8)
    grad_blocks = gaussian(key_list[0], (N_REP, NBLK, B, B), 1.0, 6.0, ((0, 4), (2, 8)))
    graft_accum = draw_graft_accum(jax.random.fold_in(key_list[7], 71), 0)
    left_stats = draw_left_stats(jax.random.fold_in(key_list[7], 71), 0)
    right_stats = draw_right_stats(jax.random.fold_in(key_list[7], 71), 0)
    block_slot = draw_block_slot(jax.random.fold_in(key_list[7], 71), 0)
    vocab_grads = gaussian(key_list[5], (N_REP, 2, VOC, D), 1.0, 6.0, ((0, 4), (2, 8)))
    vocab_accum = jnp.clip(jnp.exp(math.log(10.0) - 6.9077553 * jax.random.uniform(key_list[6], (2, VOC, D), jnp.float32) ** block_scale(key_list[6], (2, VOC, D), ((1, 8),), -0.2, 0.2)), 0.01, 10.0)
    return {"grad_blocks": grad_blocks, "graft_accum": graft_accum, "left_stats": left_stats, "right_stats": right_stats, "block_slot": block_slot, "vocab_grads": vocab_grads, "vocab_accum": vocab_accum}


def product(left, right):
    return jnp.dot(left, right, precision=lax.Precision.HIGHEST)

def inverse_root(matrix):
    identity = jnp.eye(matrix.shape[0], dtype=matrix.dtype)
    frobenius = jnp.sqrt(jnp.sum(matrix * matrix))
    scaled = matrix / frobenius
    result = identity
    for iteration in range(ITERS):
        factor = (5.0 * identity - scaled) * 0.25
        result = factor if iteration == 0 else product(result, factor)
        if iteration + 1 < ITERS:
            square = product(factor, factor)
            fourth = product(square, square)
            scaled = product(fourth, scaled)
    return result

def reference(grad_blocks, graft_accum, left_stats, right_stats, block_slot, vocab_grads, vocab_accum):
    grad_sum = lax.optimization_barrier(jnp.sum(grad_blocks.astype(jnp.float32), axis=0)).astype(jnp.bfloat16)
    vocab_sum = lax.optimization_barrier(jnp.sum(vocab_grads.astype(jnp.float32), axis=0)).astype(jnp.bfloat16)
    vocab_float = vocab_sum.astype(jnp.float32)
    vocab_accum_new = vocab_accum + vocab_float * vocab_float
    vocab_step = (vocab_float / (jnp.sqrt(vocab_accum_new) + 1e-10)).astype(jnp.bfloat16)
    grad_float = grad_sum.astype(jnp.float32)
    graft_accum_new = graft_accum + grad_float * grad_float
    grafted = grad_float / (jnp.sqrt(graft_accum_new) + 1e-10)
    graft_mean = lax.optimization_barrier(jnp.mean(grafted * grafted, axis=(1, 2)))

    def one_block(inputs):
        block_grad, slot_index, block_mean = inputs
        left_block = left_stats[slot_index] + jnp.dot(block_grad, block_grad.T, preferred_element_type=jnp.float32)
        right_block = right_stats[slot_index] + jnp.dot(block_grad.T, block_grad, preferred_element_type=jnp.float32)
        block_float = block_grad.astype(jnp.float32)
        shampoo = product(product(inverse_root(left_block), block_float), inverse_root(right_block))
        graft_scale = jnp.sqrt(block_mean) / jnp.sqrt(jnp.mean(shampoo * shampoo) + 1e-06)
        return ((shampoo * graft_scale).astype(jnp.bfloat16), left_block, right_block)
    direction, left_blocks, right_blocks = lax.map(one_block, (grad_sum, block_slot.astype(jnp.int32), graft_mean))
    left_new = left_stats.at[block_slot].set(left_blocks)
    right_new = right_stats.at[block_slot].set(right_blocks)
    return (direction, graft_accum_new, left_new, right_new, vocab_accum_new, vocab_step)
```

```python
import jax
import jax.numpy as jnp
from jax import lax
from jax.experimental import pallas as pl
from jax.experimental.pallas import tpu as pltpu
from jax.sharding import PartitionSpec as P

ITERS = 6
TAIL = 16
F32 = jnp.float32
BF16 = jnp.bfloat16
VMEM = pl.BlockSpec(memory_space=pltpu.VMEM)
SMEM = pl.BlockSpec(memory_space=pltpu.SMEM)
ANY = pl.BlockSpec(memory_space=pl.ANY)


def shape(dims, dtype):
    return jax.ShapeDtypeStruct(dims, dtype)


def call(body, outs, in_specs, scratch=(), flops=0, moved=0):
    return pl.pallas_call(
        body,
        out_shape=outs,
        in_specs=in_specs,
        out_specs=jax.tree.map(lambda _: VMEM, outs),
        scratch_shapes=list(scratch),
        compiler_params=pltpu.CompilerParams(vmem_limit_bytes=40 << 20),
        cost_estimate=pl.CostEstimate(flops=flops, bytes_accessed=moved, transcendentals=0),
    )


def dot(left, right):
    return jnp.dot(left, right, preferred_element_type=F32)


def three_terms(value):
    high = value.astype(BF16).astype(F32)
    middle = (value - high).astype(BF16).astype(F32)
    return high, middle, value - high - middle


def exchange(values, axis, mask, size):
    return lax.ppermute(values, axis, [(i, i ^ mask) for i in range(size)])


def on_device(
    grad_blocks, graft_accum, left_stats, right_stats, block_slot, vocab_grads, vocab_accum
):
    reps, indices = lax.axis_size("rep"), lax.axis_size("fsdp")
    blocks, rows, order = grad_blocks.shape[1:]
    most = left_stats.shape[0]
    planes, per, cols = indices // 2, 2 * most, order // reps
    assert per <= reps and blocks % reps == 0
    share = blocks // reps
    rep, index = lax.axis_index("rep"), lax.axis_index("fsdp")
    plane, core = index // 2, index % 2
    rep_partners, plane_partners = range(1, reps), range(1, planes)
    entries = float(order * order)

    rank = jnp.sum((block_slot[None, :] < block_slot[:, None]).astype(jnp.int32), axis=1)
    slot_plane, slot_local = block_slot // per, block_slot % per
    rep_range = jnp.arange(reps, dtype=jnp.int32)
    worker = rank % reps
    local_of = jnp.sum(
        jnp.where(
            (slot_plane[None, :] == plane) & (worker[None, :] == rep_range[:, None]),
            slot_local[None, :],
            0,
        ),
        axis=1,
    )
    place_of = (
        jnp.sum(
            jnp.where(
                (
                    slot_plane[None, :]
                    == (jnp.arange(planes, dtype=jnp.int32) ^ plane)[:, None]
                )
                & (worker[None, :] == rep),
                rank[None, :] // reps + 1,
                0,
            ),
            axis=1,
        )
        - 1
    )
    block_range = jnp.arange(blocks, dtype=jnp.int32)
    block_of = jnp.sum(
        jnp.where(rank[None, :] == block_range[:, None], block_range[None, :], 0), axis=1
    )
    here = jnp.stack([rep, plane, core]).astype(jnp.int32)
    info = jnp.concatenate([here, local_of, place_of, block_of])
    at_local, at_place, at_block = 3, 3 + reps, 3 + reps + planes

    own = grad_blocks[0]
    sent = [
        lax.dynamic_slice_in_dim(own, (rep ^ k) * cols, cols, 2) for k in range(reps)
    ]
    terms = [sent[0]] + [exchange(sent[k], "rep", k, reps) for k in rep_partners]
    accum_share = lax.dynamic_slice_in_dim(graft_accum, rep * cols, cols, 2)
    payload_rows = per * rows + TAIL

    def sum_body(here_ref, slot_ref, *refs):
        term_refs, accum_ref, sum_ref = refs[:reps], refs[reps], refs[reps + 1]
        out_refs = refs[reps + 2 : reps + 2 + planes]
        slots, parts, tail = refs[reps + 2 + planes :]
        slots[...] = jnp.zeros_like(slots)
        parts[...] = jnp.zeros_like(parts)
        for b in range(blocks):
            total = term_refs[0][b].astype(F32)
            for term in term_refs[1:]:
                total = total + term[b].astype(F32)
            summed = total.astype(BF16)
            sum_ref[b] = summed
            value = summed.astype(F32)
            grafted = value / (jnp.sqrt(accum_ref[b] + value * value) + 1e-10)
            slot = slot_ref[b]
            away = (slot // per) ^ here_ref[1]
            local = slot % per
            slots[away, local] = summed
            parts[away, pl.ds(local, 1), :] = jnp.sum(grafted * grafted, axis=0, keepdims=True)
        tail[...] = jnp.zeros_like(tail)
        for k in range(planes):
            for s in range(per):
                out_refs[k][s * rows : (s + 1) * rows, :] = slots[k, s]
            for t, term in enumerate(three_terms(parts[k, :per, :])):
                tail[t * per : (t + 1) * per, :] = term
            out_refs[k][per * rows :, :] = tail[...].astype(BF16)

    summed = call(
        sum_body,
        [shape((blocks, rows, cols), BF16)]
        + [shape((payload_rows, cols), BF16) for _ in range(planes)],
        [SMEM, SMEM] + [VMEM] * (reps + 1),
        [
            pltpu.VMEM((planes, per, rows, cols), BF16),
            pltpu.VMEM((planes, 8, cols), F32),
            pltpu.VMEM((TAIL, cols), F32),
        ],
        moved=4 * blocks * rows * order,
    )(here, block_slot, *terms, accum_share)
    grad_share, payloads = summed[0], summed[1:]

    arrived = [payloads[0]] + [
        exchange(payloads[k], "fsdp", 2 * k, indices) for k in plane_partners
    ]
    part_rows = planes * rows + TAIL

    def route_body(info_ref, *refs):
        in_refs = refs[:planes]
        out_refs = refs[planes : planes + reps]
        keep_ref, give_ref, parts, tail = refs[planes + reps :]
        rep_here, core_here = info_ref[0], info_ref[2]
        total = jnp.zeros((per, cols), F32)
        for ref in in_refs:
            bits = ref[per * rows :, :].astype(F32)
            for t in range(3):
                total = total + bits[t * per : (t + 1) * per]
        parts[:per, :] = total
        tail[...] = jnp.zeros_like(tail)
        for j in range(reps):
            local = info_ref[at_local + (rep_here ^ j)]
            for s in range(per):

                @pl.when(local == s)
                def _():
                    for k in range(planes):
                        out_refs[j][k * rows : (k + 1) * rows, :] = in_refs[k][
                            s * rows : (s + 1) * rows, :
                        ]

            for t, term in enumerate(three_terms(parts[pl.ds(local, 1), :])):
                tail[t : t + 1, :] = term
            out_refs[j][planes * rows :, :] = tail[...].astype(BF16)
        for side in range(2):

            @pl.when(core_here == side)
            def _():
                for k in range(planes):
                    for m in range(most):
                        for target, ref in ((side, keep_ref), (1 - side, give_ref)):
                            s = target * most + m
                            ref[m, k] = in_refs[k][s * rows : (s + 1) * rows, :]

    half = shape((most, planes, rows, cols), BF16)
    routed = call(
        route_body,
        [shape((part_rows, cols), BF16) for _ in range(reps)] + [half, half],
        [SMEM] + [VMEM] * planes,
        [pltpu.VMEM((8, cols), F32), pltpu.VMEM((TAIL, cols), F32)],
        moved=4 * planes * per * rows * cols * 2,
    )(info, *arrived)
    parts, keep, give = routed[:reps], routed[reps], routed[reps + 1]

    mine = jnp.stack([parts[0]] + [exchange(parts[j], "rep", j, reps) for j in rep_partners])
    other = exchange(mine, "fsdp", 1, indices)
    local_here = lax.dynamic_index_in_dim(local_of, rep, 0, keepdims=False)
    local_slot = local_here % most
    stats_sent = jnp.where(
        core == 0,
        lax.dynamic_index_in_dim(right_stats, local_slot, 0, keepdims=False),
        lax.dynamic_index_in_dim(left_stats, local_slot, 0, keepdims=False),
    )
    stats_other = exchange(stats_sent, "fsdp", 1, indices)
    scratch_type = BF16 if rows % 16 == 0 else F32

    def assemble(grad, rep_here, plane_here, core_here, piece, k, j):
        row = pl.multiple_of((2 * (plane_here ^ k) + core_here) * rows, rows)
        col = pl.multiple_of((rep_here ^ j) * cols, cols)
        grad[pl.ds(row, rows), pl.ds(col, cols)] = piece.astype(scratch_type)

    def root_body(info_ref, mine_ref, other_ref, left_ref, right_ref, stats_ref, out_ref,
                  graft_ref, grad, matrix, start, sem):
        rep_here, plane_here, core_here = info_ref[0], info_ref[1], info_ref[2]
        local = info_ref[at_local + rep_here]
        owner, at = local // most, local % most

        def fetch(source):
            return pltpu.make_async_copy(source, matrix, sem)

        @pl.when((owner == core_here) & (core_here == 0))
        def _():
            fetch(left_ref.at[at]).start()

        @pl.when((owner == core_here) & (core_here == 1))
        def _():
            fetch(right_ref.at[at]).start()

        @pl.when(owner != core_here)
        def _():
            fetch(stats_ref).start()

        graft = jnp.zeros((1, cols), F32)
        for j in range(reps):
            for ref, side in ((mine_ref, core_here), (other_ref, 1 - core_here)):
                for k in range(planes):
                    assemble(grad, rep_here, plane_here, side,
                             ref[j, k * rows : (k + 1) * rows, :], k, j)
                bits = ref[j, planes * rows :, :].astype(F32)
                graft = graft + jnp.sum(bits[:8], axis=0, keepdims=True)
        graft_ref[...] = jnp.broadcast_to(graft, graft_ref.shape)
        fetch(stats_ref).wait()

        @pl.when(core_here == 0)
        def _():
            value = grad[...].astype(BF16)
            matrix[...] += lax.dot_general(
                value, value, (((1,), (1,)), ((), ())), preferred_element_type=F32
            )
            start[...] = value.astype(F32)

        @pl.when(core_here == 1)
        def _():
            value = grad[...].astype(BF16)
            matrix[...] += lax.dot_general(
                value, value, (((0,), (0,)), ((), ())), preferred_element_type=F32
            )
            line = lax.broadcasted_iota(jnp.int32, (order, order), 0)
            start[...] = (line == lax.broadcasted_iota(jnp.int32, (order, order), 1)).astype(F32)

        scaled = matrix[...]
        scaled = scaled / jnp.sqrt(jnp.sum(scaled * scaled))
        result = start[...]
        for iteration in range(ITERS):
            low = scaled.astype(BF16)
            result = 1.25 * result - 0.25 * dot(low, result.astype(BF16))
            if iteration + 1 < ITERS:
                step = (dot(low, low) * 0.0625 - 0.625 * scaled).astype(BF16)
                twice = 1.5625 * scaled + dot(low, step)
                scaled = 1.5625 * twice + dot(twice.astype(BF16), step)
        out_ref[...] = result.astype(BF16)

    square = (order, order)
    root, graft_sum = call(
        root_body,
        [shape(square, BF16), shape((8, cols), F32)],
        [SMEM, VMEM, VMEM, ANY, ANY, ANY],
        [
            pltpu.VMEM(square, scratch_type),
            pltpu.VMEM(square, F32),
            pltpu.VMEM(square, F32),
            pltpu.SemaphoreType.DMA,
        ],
        flops=2 * 22 * order**3,
        moved=8 * order * order,
    )(info, mine, other, left_stats, right_stats, stats_other)
    root_other = exchange(root, "fsdp", 1, indices)

    def finish_body(info_ref, mine_ref, other_ref, graft_ref, *refs):
        out_refs, result = refs[:planes], refs[planes]
        plane_here, core_here = info_ref[1], info_ref[2]

        @pl.when(core_here == 0)
        def _():
            result[...] = dot(mine_ref[...], other_ref[...])

        @pl.when(core_here == 1)
        def _():
            result[...] = dot(other_ref[...], mine_ref[...])

        value = result[...]
        mean = jnp.sum(value * value) / entries
        graft_mean = jnp.sum(graft_ref[0:1, :]) / entries
        scale = jnp.sqrt(graft_mean) / jnp.sqrt(mean + 1e-06)
        for k in range(planes):
            row = pl.multiple_of((2 * (plane_here ^ k) + core_here) * rows, rows)
            out_refs[k][...] = (result[pl.ds(row, rows), :] * scale).astype(BF16)

    slabs = call(
        finish_body,
        [shape((rows, order), BF16) for _ in range(planes)],
        [SMEM, VMEM, VMEM, VMEM],
        [pltpu.VMEM(square, F32)],
        flops=2 * order**3,
        moved=6 * order * order,
    )(info, root, root_other, graft_sum)

    returned = [slabs[0]] + [
        exchange(slabs[k], "fsdp", 2 * k, indices) for k in plane_partners
    ]

    def pick_body(info_ref, *refs):
        out_ref = refs[planes]
        for k in range(planes):
            place = info_ref[at_place + k]

            @pl.when(place >= 0)
            def _():
                out_ref[place] = refs[k][...]

    picked = call(
        pick_body,
        shape((share, rows, order), BF16),
        [SMEM] + [VMEM] * planes,
        moved=4 * share * rows * order,
    )(info, *returned)
    gathered = [picked] + [exchange(picked, "rep", j, reps) for j in rep_partners]

    def place_body(info_ref, *refs):
        out_ref = refs[reps]
        for j in range(reps):
            for m in range(share):
                out_ref[info_ref[at_block + m * reps + (info_ref[0] ^ j)]] = refs[j][m]

    direction = call(
        place_body,
        shape((blocks, rows, order), BF16),
        [SMEM] + [VMEM] * reps,
        moved=4 * blocks * rows * order,
    )(info, *gathered)

    grad_shares = [grad_share] + [exchange(grad_share, "rep", j, reps) for j in rep_partners]

    def accum_body(info_ref, accum_ref, *refs):
        out_ref = refs[reps]
        for j in range(reps):
            at = pl.ds(pl.multiple_of((info_ref[0] ^ j) * cols, cols), cols)
            value = refs[j][...].astype(F32)
            out_ref[:, :, at] = accum_ref[:, :, at] + value * value

    graft_accum_new = call(
        accum_body,
        shape(graft_accum.shape, F32),
        [SMEM, VMEM] + [VMEM] * reps,
        moved=10 * blocks * rows * order,
    )(here, graft_accum, *grad_shares)

    got = exchange(give, "fsdp", 1, indices)
    pair = jnp.stack([keep, got])
    pairs = [pair] + [exchange(pair, "rep", j, reps) for j in rep_partners]

    def stats_body(info_ref, left_ref, right_ref, *refs):
        left_out, right_out, grad = refs[reps:]
        m = pl.program_id(0)
        rep_here, plane_here, core_here = info_ref[0], info_ref[1], info_ref[2]
        for j in range(reps):
            for part, side in ((0, core_here), (1, 1 - core_here)):
                for k in range(planes):
                    assemble(grad, rep_here, plane_here, side, refs[j][part, m, k], k, j)
        value = grad[...].astype(BF16)
        left_out[0] = left_ref[0] + lax.dot_general(
            value, value, (((1,), (1,)), ((), ())), preferred_element_type=F32
        )
        right_out[0] = right_ref[0] + lax.dot_general(
            value, value, (((0,), (0,)), ((), ())), preferred_element_type=F32
        )

    slot_block = pl.BlockSpec((1, order, order), lambda m: (m, 0, 0))
    left_new, right_new = pl.pallas_call(
        stats_body,
        grid=(most,),
        out_shape=[shape(left_stats.shape, F32), shape(right_stats.shape, F32)],
        in_specs=[SMEM, slot_block, slot_block] + [VMEM] * reps,
        out_specs=[slot_block, slot_block],
        scratch_shapes=[pltpu.VMEM(square, scratch_type)],
        compiler_params=pltpu.CompilerParams(vmem_limit_bytes=40 << 20),
        cost_estimate=pl.CostEstimate(
            flops=4 * most * order**3, bytes_accessed=16 * most * order * order, transcendentals=0
        ),
    )(info, left_stats, right_stats, *pairs)

    vocab_own = vocab_grads[0]
    vocab_cols = vocab_own.shape[2] // reps
    vocab_sent = [
        lax.dynamic_slice_in_dim(vocab_own, (rep ^ k) * vocab_cols, vocab_cols, 2)
        for k in range(reps)
    ]
    vocab_terms = [vocab_sent[0]] + [
        exchange(vocab_sent[k], "rep", k, reps) for k in rep_partners
    ]
    vocab_total = vocab_terms[0].astype(F32)
    for term in vocab_terms[1:]:
        vocab_total = vocab_total + term.astype(F32)
    vocab_share = vocab_total.astype(BF16)
    vocab_shares = [vocab_share] + [
        exchange(vocab_share, "rep", j, reps) for j in rep_partners
    ]

    def vocab_body(info_ref, accum_ref, *refs):
        accum_out, step_out = refs[reps:]
        for j in range(reps):
            at = pl.ds(pl.multiple_of((info_ref[0] ^ j) * vocab_cols, vocab_cols), vocab_cols)
            value = refs[j][...].astype(F32)
            accum = accum_ref[:, :, at] + value * value
            accum_out[:, :, at] = accum
            step_out[:, :, at] = (value / (jnp.sqrt(accum) + 1e-10)).astype(BF16)

    vocab_accum_new, vocab_step = call(
        vocab_body,
        [shape(vocab_accum.shape, F32), shape(vocab_accum.shape, BF16)],
        [SMEM, VMEM] + [VMEM] * reps,
        moved=6 * vocab_accum.size,
    )(here, vocab_accum, *vocab_shares)
    return (direction, graft_accum_new, left_new, right_new, vocab_accum_new, vocab_step)


def solution(mesh):
    in_specs = (
        P("rep", None, "fsdp", None),
        P(None, "fsdp", None),
        P("fsdp", None, None),
        P("fsdp", None, None),
        P(),
        P("rep", None, "fsdp", None),
        P(None, "fsdp", None),
    )
    out_specs = (
        P(None, "fsdp", None),
        P(None, "fsdp", None),
        P("fsdp", None, None),
        P("fsdp", None, None),
        P(None, "fsdp", None),
        P(None, "fsdp", None),
    )
    return jax.shard_map(
        on_device, mesh=mesh, in_specs=in_specs, out_specs=out_specs, check_vma=False
    )
```

```python
import jax
import jax.numpy as jnp
from jax import lax
from jax.experimental import pallas as pl
from jax.experimental.pallas import tpu as pltpu
from jax.sharding import PartitionSpec as P

ITERS = 6
TAIL = 16
F32 = jnp.float32
BF16 = jnp.bfloat16
VMEM = pl.BlockSpec(memory_space=pltpu.VMEM)
SMEM = pl.BlockSpec(memory_space=pltpu.SMEM)
ANY = pl.BlockSpec(memory_space=pl.ANY)
HBM = pl.BlockSpec(memory_space=pltpu.HBM)
MIB = 1 << 20
LONG = 4 * 10**9


def shape(dims, dtype):
    return jax.ShapeDtypeStruct(dims, dtype)


def call(body, outs, in_specs, out_specs=None, scratch=(), flops=1, vmem=8):
    return pl.pallas_call(
        body,
        out_shape=outs,
        in_specs=in_specs,
        out_specs=jax.tree.map(lambda _: VMEM, outs) if out_specs is None else out_specs,
        scratch_shapes=list(scratch),
        compiler_params=pltpu.CompilerParams(vmem_limit_bytes=vmem * MIB),
        cost_estimate=pl.CostEstimate(flops=flops, bytes_accessed=1, transcendentals=0),
    )


def dot(left, right):
    return jnp.dot(left, right, preferred_element_type=F32)


def gram(value, axis):
    return lax.dot_general(
        value, value, (((axis,), (axis,)), ((), ())), preferred_element_type=F32
    )


def three_terms(value):
    high = value.astype(BF16).astype(F32)
    middle = (value - high).astype(BF16).astype(F32)
    return high, middle, value - high - middle


def exchange(values, axis, mask, size):
    return lax.ppermute(values, axis, [(i, i ^ mask) for i in range(size)])


def fence(arrays, *done, flops=1):
    def body(*refs):
        pass

    return pl.pallas_call(
        body,
        out_shape=[shape(array.shape, array.dtype) for array in arrays],
        in_specs=[ANY] * (len(arrays) + len(done)),
        out_specs=[ANY] * len(arrays),
        input_output_aliases={i: i for i in range(len(arrays))},
        compiler_params=pltpu.CompilerParams(vmem_limit_bytes=MIB),
        cost_estimate=pl.CostEstimate(flops=flops, bytes_accessed=1, transcendentals=0),
    )(*arrays, *done)


def late(arrays, *done):
    return fence(fence(arrays, flops=LONG), *done)


def in_hbm(array):
    return pltpu.with_memory_space_constraint(array, pltpu.HBM)


def place():
    index = lax.axis_index("fsdp")
    return lax.axis_index("rep"), index // 2, index % 2


def on_device(
    grad_blocks, graft_accum, left_stats, right_stats, block_slot, vocab_grads, vocab_accum
):
    reps, indices = lax.axis_size("rep"), lax.axis_size("fsdp")
    blocks, rows, order = grad_blocks.shape[1:]
    most = left_stats.shape[0]
    planes, per, cols = indices // 2, 2 * most, order // reps
    assert per <= reps and blocks % reps == 0
    share, slots = blocks // reps, per * planes
    rep_partners, plane_partners = range(1, reps), range(1, planes)
    entries = float(order * order)
    square = (order, order)
    scratch_type = BF16 if rows % 16 == 0 else F32
    vocab_own = vocab_grads[0]
    vocab_cols = vocab_own.shape[2] // reps
    grad_rows, pair_rows = blocks * rows, vocab_own.shape[0] * vocab_own.shape[1]
    chunks = vocab_cols // cols
    vocab_rows = chunks * pair_rows
    share_rows = (grad_rows + vocab_rows) // 2
    assert share_rows % rows == 0 and share_rows % pair_rows == 0
    assert reps == 4 and most == 2
    ways = ((1, 2), (2, 1))
    right_other = exchange(right_stats, "fsdp", 1, indices)

    def ranked(slot_ref, who, visit):
        for s in range(slots):
            who[s] = -1
        for b in range(blocks):
            who[slot_ref[0, b]] = b
        count = jnp.int32(0)
        for s in range(slots):
            block = who[s]
            visit(s, block, count)
            count = count + jnp.where(block >= 0, 1, 0)

    def local_slots(slot_ref, who, local_of):
        plane_here = place()[1]
        for j in range(reps):
            local_of[j] = 0

        def visit(s, block, count):
            @pl.when((block >= 0) & (plane_here == s // per))
            def _():
                local_of[count % reps] = s % per

        ranked(slot_ref, who, visit)

    def cut_body(slot_ref, grad_ref, vocab_ref, *refs):
        out_refs, table_ref = refs[:reps], refs[reps]
        line = lax.broadcasted_iota(jnp.int32, table_ref.shape, 1)
        table = jnp.zeros(table_ref.shape, jnp.int32)
        for b in range(blocks):
            table = jnp.where(line == b, slot_ref[b], table)
        table_ref[...] = table
        for k in range(reps):
            part = place()[0] ^ k
            at = pl.ds(pl.multiple_of(part * cols, cols), cols)
            for b in range(blocks):
                out_refs[k][b * rows : (b + 1) * rows, :] = grad_ref[b, :, at]
            at = pl.ds(pl.multiple_of(part * vocab_cols, vocab_cols), vocab_cols)
            value = vocab_ref[:, :, at].astype(F32).reshape(pair_rows, vocab_cols).astype(BF16)
            for i in range(chunks):
                first = grad_rows + i * pair_rows
                out_refs[k][first : first + pair_rows, :] = value[:, i * cols : (i + 1) * cols]

    cut = call(
        cut_body,
        [shape((grad_rows + vocab_rows, cols), BF16)] * reps
        + [shape((1, 128), jnp.int32)],
        [SMEM, VMEM, VMEM],
        vmem=8,
    )(in_hbm(block_slot), in_hbm(grad_blocks[0]), in_hbm(vocab_own))
    pieces, table = cut[:reps], cut[reps]
    accum_share = lax.dynamic_slice_in_dim(
        graft_accum, lax.axis_index("rep") * cols, cols, 2
    )

    terms = [pieces[0]] + [exchange(pieces[k], "rep", k, reps) for k in rep_partners]
    payload_rows = per * rows + TAIL

    book = [pltpu.SMEM((slots,), jnp.int32), pltpu.SMEM((reps,), jnp.int32)]

    def sum_body(slot_ref, *refs):
        term_refs, accum_ref, share_refs = refs[:reps], refs[reps], refs[reps + 1 : reps + 3]
        out_refs = refs[reps + 3 : reps + 3 + planes]
        held, parts, tail = refs[reps + 3 + planes :]
        plane_here = place()[1]

        def total_of(first, count):
            total = term_refs[0][first : first + count, :].astype(F32)
            for term in term_refs[1:]:
                total = total + term[first : first + count, :].astype(F32)
            return total.astype(BF16)

        def keep(first, value):
            half, at = first // share_rows, first % share_rows
            share_refs[half][at : at + value.shape[0], :] = value

        for i in range(chunks):
            first = grad_rows + i * pair_rows
            keep(first, total_of(first, pair_rows))
        held[...] = jnp.zeros_like(held)
        parts[...] = jnp.zeros_like(parts)
        for b in range(blocks):
            summed = total_of(b * rows, rows)
            keep(b * rows, summed)
            value = summed.astype(F32)
            grafted = value / (jnp.sqrt(accum_ref[b] + value * value) + 1e-10)
            slot = slot_ref[0, b]
            away = (slot // per) ^ plane_here
            local = slot % per
            held[away, local] = summed
            parts[away, pl.ds(local, 1), :] = jnp.sum(grafted * grafted, axis=0, keepdims=True)
        tail[...] = jnp.zeros_like(tail)
        for k in range(planes):
            for s in range(per):
                out_refs[k][s * rows : (s + 1) * rows, :] = held[k, s]
            for t, term in enumerate(three_terms(parts[k, :per, :])):
                tail[t * per : (t + 1) * per, :] = term
            out_refs[k][per * rows :, :] = tail[...].astype(BF16)

    summed = call(
        sum_body,
        [shape((share_rows, cols), BF16)] * 2
        + [shape((payload_rows, cols), BF16)] * planes,
        [SMEM] + [VMEM] * (reps + 1),
        scratch=[
            pltpu.VMEM((planes, per, rows, cols), BF16),
            pltpu.VMEM((planes, 8, cols), F32),
            pltpu.VMEM((TAIL, cols), F32),
        ],
    )(table, *terms, accum_share)
    shares, payloads = summed[:2], summed[2:]

    arrived = [payloads[0]] + [
        exchange(payloads[k], "fsdp", 2 * k, indices) for k in plane_partners
    ]

    share_firsts = [exchange(shares[m], "rep", ways[m][0], reps) for m in range(2)]
    part_rows = planes * rows + TAIL

    def route_body(slot_ref, *refs):
        in_refs = refs[:planes]
        out_refs = refs[planes : planes + reps]
        half_refs = refs[planes + reps : planes + reps + most]
        parts, tail, who, local_of = refs[planes + reps + most :]
        rep_here = place()[0]
        local_slots(slot_ref, who, local_of)
        total = jnp.zeros((per, cols), F32)
        for ref in in_refs:
            bits = ref[per * rows :, :].astype(F32)
            for t in range(3):
                total = total + bits[t * per : (t + 1) * per]
        parts[:per, :] = total
        tail[...] = jnp.zeros_like(tail)
        for j in range(reps):
            local = local_of[rep_here ^ j]
            for s in range(per):

                @pl.when(local == s)
                def _():
                    for k in range(planes):
                        out_refs[j][k * rows : (k + 1) * rows, :] = in_refs[k][
                            s * rows : (s + 1) * rows, :
                        ]

            for t, term in enumerate(three_terms(parts[pl.ds(local, 1), :])):
                tail[t : t + 1, :] = term
            out_refs[j][planes * rows :, :] = tail[...].astype(BF16)
        for k in range(planes):
            for m in range(most):
                for side in range(2):
                    s = side * most + m
                    at = (side * planes + k) * rows
                    half_refs[m][at : at + rows, :] = in_refs[k][s * rows : (s + 1) * rows, :]

    half = shape((2 * planes * rows, cols), BF16)
    routed = call(
        route_body,
        [shape((part_rows, cols), BF16)] * reps + [half] * most,
        [SMEM] + [VMEM] * planes,
        scratch=[pltpu.VMEM((8, cols), F32), pltpu.VMEM((TAIL, cols), F32)] + book,
    )(table, *arrived)
    routed = late(routed, *share_firsts, right_other)
    parts, halves = routed[:reps], routed[reps:]

    met = [parts[0]] + [exchange(parts[j], "rep", j, reps) for j in rep_partners]
    firsts = [exchange(halves[m], "rep", ways[m][0], reps) for m in range(2)]
    mine = late([jnp.stack(met)], *firsts)[0]
    other = exchange(mine, "fsdp", 1, indices)
    half_rows = 2 * planes * rows
    lasts = []
    for m in range(2):
        arrays = (halves[m], firsts[m], shares[m], share_firsts[m])
        joined = jnp.concatenate([array.reshape(-1, cols) for array in arrays])
        lasts.append(exchange(fence([joined], mine)[0], "rep", ways[m][1], reps))

    def assemble(grad, rep_here, plane_here, core_here, piece, k, j):
        row = pl.multiple_of((2 * (plane_here ^ k) + core_here) * rows, rows)
        col = pl.multiple_of((rep_here ^ j) * cols, cols)
        grad[pl.ds(row, rows), pl.ds(col, cols)] = piece.astype(scratch_type)

    def root_body(slot_ref, mine_ref, other_ref, left_ref, right_ref,
                  out_ref, graft_ref, grad, matrix, start, who, local_of, sem):
        rep_here, plane_here, core_here = place()
        local_slots(slot_ref, who, local_of)
        owner, at = local_of[rep_here] // most, local_of[rep_here] % most

        @pl.when(owner == core_here)
        def _():
            pltpu.make_async_copy(left_ref.at[at], matrix, sem).start()

        @pl.when(owner != core_here)
        def _():
            pltpu.make_async_copy(right_ref.at[at], matrix, sem).start()

        graft = jnp.zeros((1, cols), F32)
        for j in range(reps):
            for ref, side in ((mine_ref, core_here), (other_ref, 1 - core_here)):
                for k in range(planes):
                    assemble(grad, rep_here, plane_here, side,
                             ref[j, k * rows : (k + 1) * rows, :], k, j)
                bits = ref[j, planes * rows :, :].astype(F32)
                graft = graft + jnp.sum(bits[:8], axis=0, keepdims=True)
        line = lax.broadcasted_iota(jnp.int32, graft_ref.shape, 0)
        first = jnp.where(owner == core_here, 1.0, 0.0)
        graft_ref[...] = jnp.where(line == 0, jnp.broadcast_to(graft, graft_ref.shape), first)
        pltpu.make_async_copy(left_ref.at[at], matrix, sem).wait()

        @pl.when(owner == core_here)
        def _():
            value = grad[...].astype(BF16)
            matrix[...] += gram(value, 1)
            start[...] = value.astype(F32)

        @pl.when(owner != core_here)
        def _():
            matrix[...] += gram(grad[...].astype(BF16), 0)
            line = lax.broadcasted_iota(jnp.int32, square, 0)
            start[...] = (line == lax.broadcasted_iota(jnp.int32, square, 1)).astype(F32)

        scaled = matrix[...]
        scaled = scaled / jnp.sqrt(jnp.sum(scaled * scaled))
        result = start[...]
        for iteration in range(ITERS):
            low = scaled.astype(BF16)
            result = 1.25 * result - 0.25 * dot(low, result.astype(BF16))
            if iteration + 1 < ITERS:
                step = (dot(low, low) * 0.0625 - 0.625 * scaled).astype(BF16)
                twice = 1.5625 * scaled + dot(low, step)
                scaled = 1.5625 * twice + dot(twice.astype(BF16), step)
        out_ref[...] = result.astype(BF16)

    root, graft_sum = call(
        root_body,
        [shape(square, BF16), shape((8, cols), F32)],
        [SMEM, VMEM, VMEM, ANY, ANY],
        scratch=[
            pltpu.VMEM(square, scratch_type),
            pltpu.VMEM(square, F32),
            pltpu.VMEM(square, F32),
        ]
        + book
        + [pltpu.SemaphoreType.DMA],
        flops=1,
        vmem=20,
    )(table, mine, other, left_stats, right_other)
    root = fence([root], *lasts)[0]
    root_other = exchange(root, "fsdp", 1, indices)

    def finish_body(mine_ref, other_ref, graft_ref, *refs):
        out_refs, result = refs[:planes], refs[planes]
        _, plane_here, core_here = place()
        left_here = jnp.sum(graft_ref[1:2, :]) > 0.5

        @pl.when(left_here)
        def _():
            result[...] = dot(mine_ref[...], other_ref[...])

        @pl.when(jnp.logical_not(left_here))
        def _():
            result[...] = dot(other_ref[...], mine_ref[...])

        value = result[...]
        mean = jnp.sum(value * value) / entries
        graft_mean = jnp.sum(graft_ref[0:1, :]) / entries
        scale = jnp.sqrt(graft_mean) / jnp.sqrt(mean + 1e-06)
        for k in range(planes):
            row = pl.multiple_of((2 * (plane_here ^ k) + core_here) * rows, rows)
            out_refs[k][...] = (result[pl.ds(row, rows), :] * scale).astype(BF16)

    slabs = call(
        finish_body,
        [shape((rows, order), BF16)] * planes,
        [VMEM, VMEM, VMEM],
        scratch=[pltpu.VMEM(square, F32)],
        flops=2 * order**3,
    )(root, root_other, graft_sum)

    def side_body(*refs):
        keep_ref, give_ref = refs[6:]
        core_here = place()[2]
        side_rows = planes * rows
        for m in range(2):
            own_ref, first_ref, last_ref = refs[m], refs[2 + m], refs[4 + m]
            near, far = ways[m]
            places = (
                (0, own_ref, 0),
                (near, first_ref, 0),
                (far, last_ref, 0),
                (near ^ far, last_ref, half_rows),
            )
            for j, ref, at in places:
                for target, side in ((keep_ref, core_here), (give_ref, 1 - core_here)):
                    first = pl.multiple_of(at + side * side_rows, side_rows)
                    target[j, m] = ref[pl.ds(first, side_rows), :]

    side = shape((reps, most, planes * rows, cols), BF16)
    keep, give = call(side_body, [side, side], [VMEM] * 6)(*halves, *firsts, *lasts)
    other_side = exchange(give, "fsdp", 1, indices)
    slabs = fence(slabs, other_side)

    returned = [slabs[0]] + [
        exchange(slabs[k], "fsdp", 2 * k, indices) for k in plane_partners
    ]

    def stats_body(left_ref, right_ref, after_ref, keep_ref, other_ref,
                   left_out, right_out, token_ref, grad):
        m = pl.program_id(0)
        token_ref[...] = jnp.zeros_like(token_ref)
        rep_here, plane_here, core_here = place()
        for j in range(reps):
            for ref, side in ((keep_ref, core_here), (other_ref, 1 - core_here)):
                for k in range(planes):
                    assemble(grad, rep_here, plane_here, side,
                             ref[j, m, k * rows : (k + 1) * rows, :], k, j)
        value = grad[...].astype(BF16)
        left_out[0] = left_ref[0] + gram(value, 1)
        right_out[0] = right_ref[0] + gram(value, 0)

    token = shape((8, 128), F32)
    slot_block = pl.BlockSpec((1, order, order), lambda m: (m, 0, 0))
    left_new, right_new, stats_token = pl.pallas_call(
        stats_body,
        grid=(most,),
        out_shape=[shape(left_stats.shape, F32), shape(right_stats.shape, F32), token],
        in_specs=[slot_block, slot_block, ANY, VMEM, VMEM],
        out_specs=[slot_block, slot_block, pl.BlockSpec((8, 128), lambda m: (0, 0))],
        scratch_shapes=[pltpu.VMEM(square, scratch_type)],
        compiler_params=pltpu.CompilerParams(vmem_limit_bytes=20 * MIB),
        cost_estimate=pl.CostEstimate(
            flops=1, bytes_accessed=1, transcendentals=0
        ),
    )(left_stats, right_stats, slabs[0], keep, other_side)

    def pick_body(slot_ref, *refs):
        out_ref, who = refs[-2:]
        rep_here, plane_here, _ = place()

        def visit(s, block, count):
            @pl.when((block >= 0) & (count % reps == rep_here))
            def _():
                for k in range(planes):

                    @pl.when(plane_here == (s // per) ^ k)
                    def _():
                        out_ref[count // reps] = refs[k][...]

        ranked(slot_ref, who, visit)

    picked = call(
        pick_body,
        shape((share, rows, order), BF16),
        [SMEM] + [VMEM] * planes + [ANY],
        scratch=book[:1],
    )(table, *returned, stats_token)
    gathered = [picked] + [exchange(picked, "rep", j, reps) for j in rep_partners]

    def accum_body(accum_ref, vocab_ref, after_ref, *refs):

        def piece(j, first, count):
            m, at = first // share_rows, first % share_rows
            near, far = ways[m]
            ref, base = {
                0: (refs[m], 0),
                near: (refs[2 + m], 0),
                far: (refs[4 + m], 2 * half_rows),
                near ^ far: (refs[4 + m], 2 * half_rows + share_rows),
            }[j]
            return ref[base + at : base + at + count, :].astype(F32)

        accum_out, vocab_out, step_out, token_ref = refs[6:]
        token_ref[...] = jnp.zeros_like(token_ref)
        rep_here = place()[0]
        for j in range(reps):
            at = pl.ds(pl.multiple_of((rep_here ^ j) * cols, cols), cols)
            for b in range(blocks):
                value = piece(j, b * rows, rows)
                accum_out[b, :, at] = accum_ref[b, :, at] + value * value
            for i in range(chunks):
                value = piece(j, grad_rows + i * pair_rows, pair_rows)
                value = value.reshape(vocab_own.shape[:2] + (cols,))
                start = pl.multiple_of((rep_here ^ j) * vocab_cols + i * cols, cols)
                at_vocab = pl.ds(start, cols)
                accum = vocab_ref[:, :, at_vocab] + value * value
                vocab_out[:, :, at_vocab] = accum
                step_out[:, :, at_vocab] = (value / (jnp.sqrt(accum) + 1e-10)).astype(BF16)

    graft_accum_new, vocab_accum_new, vocab_step, accum_token = call(
        accum_body,
        [
            shape(graft_accum.shape, F32),
            shape(vocab_accum.shape, F32),
            shape(vocab_accum.shape, BF16),
            token,
        ],
        [VMEM, VMEM, ANY] + [VMEM] * 6,
        vmem=12,
    )(graft_accum, vocab_accum, picked, *shares, *share_firsts, *lasts)

    def place_body(slot_ref, *refs):
        out_ref, who, block_of, sem = refs[reps + 1 :]
        rep_here = place()[0]

        def visit(s, block, count):
            @pl.when(block >= 0)
            def _():
                block_of[count] = block

        ranked(slot_ref, who, visit)
        copies = []
        for j in range(reps):
            for m in range(share):
                block = block_of[m * reps + (rep_here ^ j)]
                copies.append(
                    pltpu.make_async_copy(
                        refs[j].at[m], out_ref.at[block], sem.at[j * share + m]
                    )
                )
                copies[-1].start()
        for copy in copies:
            copy.wait()

    direction = call(
        place_body,
        shape((blocks, rows, order), BF16),
        [SMEM] + [VMEM] * reps + [ANY],
        out_specs=HBM,
        scratch=[
            book[0],
            pltpu.SMEM((blocks,), jnp.int32),
            pltpu.SemaphoreType.DMA((blocks,)),
        ],
    )(table, *gathered, accum_token)
    return (direction, graft_accum_new, left_new, right_new, vocab_accum_new, vocab_step)


def solution(mesh):
    in_specs = (
        P("rep", None, "fsdp", None),
        P(None, "fsdp", None),
        P("fsdp", None, None),
        P("fsdp", None, None),
        P(),
        P("rep", None, "fsdp", None),
        P(None, "fsdp", None),
    )
    out_specs = (
        P(None, "fsdp", None),
        P(None, "fsdp", None),
        P("fsdp", None, None),
        P("fsdp", None, None),
        P(None, "fsdp", None),
        P(None, "fsdp", None),
    )
    return jax.shard_map(
        on_device, mesh=mesh, in_specs=in_specs, out_specs=out_specs, check_vma=False
    )
```

```python
import jax
import jax.numpy as jnp
from jax import lax
from jax.experimental import pallas as pl
from jax.experimental.pallas import tpu as pltpu
from jax.sharding import PartitionSpec as P

ITERS = 6
TAIL = 16
F32 = jnp.float32
BF16 = jnp.bfloat16
VMEM = pl.BlockSpec(memory_space=pltpu.VMEM)
SMEM = pl.BlockSpec(memory_space=pltpu.SMEM)
ANY = pl.BlockSpec(memory_space=pl.ANY)
HBM = pl.BlockSpec(memory_space=pltpu.HBM)
MIB = 1 << 20
LONG = 4 * 10**9
SWAP = 1


def shape(dims, dtype):
    return jax.ShapeDtypeStruct(dims, dtype)


def call(body, outs, in_specs, out_specs=None, scratch=(), flops=1, vmem=8):
    return pl.pallas_call(
        body,
        out_shape=outs,
        in_specs=in_specs,
        out_specs=jax.tree.map(lambda _: VMEM, outs) if out_specs is None else out_specs,
        scratch_shapes=list(scratch),
        compiler_params=pltpu.CompilerParams(vmem_limit_bytes=vmem * MIB),
        cost_estimate=pl.CostEstimate(flops=flops, bytes_accessed=1, transcendentals=0),
    )


def dot(left, right):
    return jnp.dot(left, right, preferred_element_type=F32)


def gram(value, axis):
    return lax.dot_general(
        value, value, (((axis,), (axis,)), ((), ())), preferred_element_type=F32
    )


def three_terms(value):
    high = value.astype(BF16).astype(F32)
    middle = (value - high).astype(BF16).astype(F32)
    return high, middle, value - high - middle


def exchange(values, axis, mask, size):
    return lax.ppermute(values, axis, [(i, i ^ mask) for i in range(size)])


def fence(arrays, *done, flops=1):
    def body(*refs):
        pass

    return pl.pallas_call(
        body,
        out_shape=[shape(array.shape, array.dtype) for array in arrays],
        in_specs=[ANY] * (len(arrays) + len(done)),
        out_specs=[ANY] * len(arrays),
        input_output_aliases={i: i for i in range(len(arrays))},
        compiler_params=pltpu.CompilerParams(vmem_limit_bytes=MIB),
        cost_estimate=pl.CostEstimate(flops=flops, bytes_accessed=1, transcendentals=0),
    )(*arrays, *done)


def late(arrays, *done):
    return fence(fence(arrays, flops=LONG), *done)


def in_hbm(array):
    return pltpu.with_memory_space_constraint(array, pltpu.HBM)


def place():
    index = lax.axis_index("fsdp")
    return lax.axis_index("rep"), index // 2, index % 2


def on_device(
    grad_blocks, graft_accum, left_stats, right_stats, block_slot, vocab_grads, vocab_accum
):
    reps, indices = lax.axis_size("rep"), lax.axis_size("fsdp")
    blocks, rows, order = grad_blocks.shape[1:]
    most = left_stats.shape[0]
    planes, per, cols = indices // 2, 2 * most, order // reps
    assert per <= reps and blocks % reps == 0
    share, slots = blocks // reps, per * planes
    rep_partners, plane_partners = range(1, reps), range(1, planes)
    entries = float(order * order)
    square = (order, order)
    scratch_type = BF16 if rows % 16 == 0 else F32
    vocab_own = vocab_grads[0]
    vocab_cols = vocab_own.shape[2] // reps
    grad_rows, pair_rows = blocks * rows, vocab_own.shape[0] * vocab_own.shape[1]
    chunks = vocab_cols // cols
    vocab_rows = chunks * pair_rows
    share_rows = (grad_rows + vocab_rows) // 2
    assert share_rows % rows == 0 and share_rows % pair_rows == 0
    assert reps == 4 and most == 2
    ways = ((1, 2), (2, 1))
    right_other = exchange(right_stats, "fsdp", 1, indices)

    def ranked(slot_ref, who, visit):
        for s in range(slots):
            who[s] = -1
        for b in range(blocks):
            who[slot_ref[0, b]] = b
        count = jnp.int32(0)
        for s in range(slots):
            block = who[s]
            visit(s, block, count)
            count = count + jnp.where(block >= 0, 1, 0)

    at_local, at_place, at_block = 0, reps, reps + planes
    width = -(-(at_block + blocks) // 128) * 128

    def book_body(slot_ref, out_ref, who):
        rep_here, plane_here, _ = place()
        line = lax.broadcasted_iota(jnp.int32, out_ref.shape, 1)
        out_ref[...] = jnp.where((line >= at_place) & (line < at_block), -1, 0)

        def visit(s, block, count):
            @pl.when(block >= 0)
            def _():
                entry = out_ref[...]
                here = (plane_here == s // per) & (line == at_local + count % reps)
                entry = jnp.where(here, s % per, entry)
                near = (count % reps == rep_here) & (
                    line == at_place + (plane_here ^ (s // per))
                )
                entry = jnp.where(near, count // reps, entry)
                out_ref[...] = jnp.where(line == at_block + count, block, entry)

        ranked(slot_ref, who, visit)

    def cut_body(slot_ref, grad_ref, vocab_ref, *refs):
        out_refs, table_ref = refs[:reps], refs[reps]
        line = lax.broadcasted_iota(jnp.int32, table_ref.shape, 1)
        table = jnp.zeros(table_ref.shape, jnp.int32)
        for b in range(blocks):
            table = jnp.where(line == b, slot_ref[b], table)
        table_ref[...] = table
        for k in range(reps):
            part = place()[0] ^ k
            at = pl.ds(pl.multiple_of(part * cols, cols), cols)
            for b in range(blocks):
                out_refs[k][b * rows : (b + 1) * rows, :] = grad_ref[b, :, at]
            at = pl.ds(pl.multiple_of(part * vocab_cols, vocab_cols), vocab_cols)
            value = vocab_ref[:, :, at].astype(F32).reshape(pair_rows, vocab_cols).astype(BF16)
            for i in range(chunks):
                first = grad_rows + i * pair_rows
                out_refs[k][first : first + pair_rows, :] = value[:, i * cols : (i + 1) * cols]

    cut = call(
        cut_body,
        [shape((grad_rows + vocab_rows, cols), BF16)] * reps
        + [shape((1, 128), jnp.int32)],
        [SMEM, VMEM, VMEM],
        vmem=8,
    )(in_hbm(block_slot), in_hbm(grad_blocks[0]), in_hbm(vocab_own))
    pieces, table = cut[:reps], cut[reps]
    accum_share = lax.dynamic_slice_in_dim(
        graft_accum, lax.axis_index("rep") * cols, cols, 2
    )

    terms = [pieces[0]] + [exchange(pieces[k], "rep", k, reps) for k in rep_partners]
    payload_rows = per * rows + TAIL

    book = call(
        book_body,
        shape((1, width), jnp.int32),
        [SMEM],
        scratch=[pltpu.SMEM((slots,), jnp.int32)],
    )(table)

    def sum_body(slot_ref, *refs):
        term_refs, accum_ref, share_refs = refs[:reps], refs[reps], refs[reps + 1 : reps + 3]
        out_refs = refs[reps + 3 : reps + 3 + planes]
        held, parts, tail = refs[reps + 3 + planes :]
        plane_here = place()[1]

        def total_of(first, count):
            total = term_refs[0][first : first + count, :].astype(F32)
            for term in term_refs[1:]:
                total = total + term[first : first + count, :].astype(F32)
            return total.astype(BF16)

        def keep(first, value):
            half, at = first // share_rows, first % share_rows
            share_refs[half][at : at + value.shape[0], :] = value

        for i in range(chunks):
            first = grad_rows + i * pair_rows
            keep(first, total_of(first, pair_rows))
        held[...] = jnp.zeros_like(held)
        parts[...] = jnp.zeros_like(parts)
        for b in range(blocks):
            summed = total_of(b * rows, rows)
            keep(b * rows, summed)
            value = summed.astype(F32)
            grafted = value / (jnp.sqrt(accum_ref[b] + value * value) + 1e-10)
            slot = slot_ref[0, b]
            away = (slot // per) ^ plane_here
            local = slot % per
            held[away, local] = summed
            parts[away, pl.ds(local, 1), :] = jnp.sum(grafted * grafted, axis=0, keepdims=True)
        tail[...] = jnp.zeros_like(tail)
        for k in range(planes):
            for s in range(per):
                out_refs[k][s * rows : (s + 1) * rows, :] = held[k, s]
            for t, term in enumerate(three_terms(parts[k, :per, :])):
                tail[t * per : (t + 1) * per, :] = term
            out_refs[k][per * rows :, :] = tail[...].astype(BF16)

    summed = call(
        sum_body,
        [shape((share_rows, cols), BF16)] * 2
        + [shape((payload_rows, cols), BF16)] * planes,
        [SMEM] + [VMEM] * (reps + 1),
        scratch=[
            pltpu.VMEM((planes, per, rows, cols), BF16),
            pltpu.VMEM((planes, 8, cols), F32),
            pltpu.VMEM((TAIL, cols), F32),
        ],
    )(table, *terms, accum_share)
    shares, payloads = summed[:2], summed[2:]

    arrived = [payloads[0]] + [
        exchange(payloads[k], "fsdp", 2 * k, indices) for k in plane_partners
    ]

    share_firsts = [exchange(shares[m], "rep", ways[m][0], reps) for m in range(2)]
    part_rows = planes * rows + TAIL

    def route_body(slot_ref, *refs):
        in_refs = refs[:planes]
        out_refs = refs[planes : planes + reps]
        whole_ref, rest_refs = refs[planes + reps], refs[planes + reps + 1 : planes + 2 * reps]
        parts, tail = refs[planes + 2 * reps :]
        rep_here = place()[0]
        total = jnp.zeros((per, cols), F32)
        for ref in in_refs:
            bits = ref[per * rows :, :].astype(F32)
            for t in range(3):
                total = total + bits[t * per : (t + 1) * per]
        parts[:per, :] = total
        tail[...] = jnp.zeros_like(tail)
        for j in range(reps):
            local = slot_ref[0, at_local + (rep_here ^ j)]
            for s in range(per):

                @pl.when(local == s)
                def _():
                    for k in range(planes):
                        out_refs[j][k * rows : (k + 1) * rows, :] = in_refs[k][
                            s * rows : (s + 1) * rows, :
                        ]

            for t, term in enumerate(three_terms(parts[pl.ds(local, 1), :])):
                tail[t : t + 1, :] = term
            out_refs[j][planes * rows :, :] = tail[...].astype(BF16)
        piece = planes * rows
        for k in range(planes):
            for s in range(per):
                at = s * piece + k * rows
                whole_ref[at : at + rows, :] = in_refs[k][s * rows : (s + 1) * rows, :]
        for j in rep_partners:
            for i in range(per - 1):
                first = (slot_ref[0, at_local + (rep_here ^ j)] + 1 + i) % per * piece
                rest_refs[j - 1][i * piece : (i + 1) * piece, :] = whole_ref[
                    pl.ds(pl.multiple_of(first, piece), piece), :
                ]

    piece_rows = planes * rows
    routed = call(
        route_body,
        [shape((part_rows, cols), BF16)] * reps
        + [shape((per * piece_rows, cols), BF16)]
        + [shape(((per - 1) * piece_rows, cols), BF16)] * (reps - 1),
        [SMEM] + [VMEM] * planes,
        scratch=[pltpu.VMEM((8, cols), F32), pltpu.VMEM((TAIL, cols), F32)],
    )(book, *arrived)
    routed = late(routed, *share_firsts, right_other)
    parts, whole, rests = routed[:reps], routed[reps], routed[reps + 1 :]

    met = [parts[0]] + [exchange(parts[j], "rep", j, reps) for j in rep_partners]
    mine = [jnp.stack(met[i : i + SWAP]) for i in range(0, reps, SWAP)]
    other = [exchange(array, "fsdp", 1, indices) for array in mine]

    rests_met = [exchange(rests[j - 1], "rep", j, reps) for j in rep_partners]

    def assemble(grad, rep_here, plane_here, core_here, piece, k, j):
        row = pl.multiple_of((2 * (plane_here ^ k) + core_here) * rows, rows)
        col = pl.multiple_of((rep_here ^ j) * cols, cols)
        grad[pl.ds(row, rows), pl.ds(col, cols)] = piece.astype(scratch_type)

    swaps = len(mine)

    def root_body(slot_ref, *refs):
        mine_refs, other_refs = refs[:swaps], refs[swaps : 2 * swaps]
        left_ref, right_ref, out_ref, graft_ref, grad, matrix, start, sem = refs[2 * swaps :]
        rep_here, plane_here, core_here = place()
        local = slot_ref[0, at_local + rep_here]
        owner, at = local // most, local % most

        @pl.when(owner == core_here)
        def _():
            pltpu.make_async_copy(left_ref.at[at], matrix, sem).start()

        @pl.when(owner != core_here)
        def _():
            pltpu.make_async_copy(right_ref.at[at], matrix, sem).start()

        graft = jnp.zeros((1, cols), F32)
        for j in range(reps):
            for swap_refs, side in ((mine_refs, core_here), (other_refs, 1 - core_here)):
                ref = swap_refs[j // SWAP].at[j % SWAP]
                for k in range(planes):
                    assemble(grad, rep_here, plane_here, side,
                             ref[k * rows : (k + 1) * rows, :], k, j)
                bits = ref[planes * rows :, :].astype(F32)
                graft = graft + jnp.sum(bits[:8], axis=0, keepdims=True)
        line = lax.broadcasted_iota(jnp.int32, graft_ref.shape, 0)
        first = jnp.where(owner == core_here, 1.0, 0.0)
        graft_ref[...] = jnp.where(line == 0, jnp.broadcast_to(graft, graft_ref.shape), first)
        pltpu.make_async_copy(left_ref.at[at], matrix, sem).wait()

        @pl.when(owner == core_here)
        def _():
            value = grad[...].astype(BF16)
            matrix[...] += gram(value, 1)
            start[...] = value.astype(F32)

        @pl.when(owner != core_here)
        def _():
            matrix[...] += gram(grad[...].astype(BF16), 0)
            line = lax.broadcasted_iota(jnp.int32, square, 0)
            start[...] = (line == lax.broadcasted_iota(jnp.int32, square, 1)).astype(F32)

        scaled = matrix[...]
        scaled = scaled / jnp.sqrt(jnp.sum(scaled * scaled))
        result = start[...]
        for iteration in range(ITERS):
            low = scaled.astype(BF16)
            result = 1.25 * result - 0.25 * dot(low, result.astype(BF16))
            if iteration + 1 < ITERS:
                step = (dot(low, low) * 0.0625 - 0.625 * scaled).astype(BF16)
                twice = 1.5625 * scaled + dot(low, step)
                scaled = 1.5625 * twice + dot(twice.astype(BF16), step)
        out_ref[...] = result.astype(BF16)

    root, graft_sum = call(
        root_body,
        [shape(square, BF16), shape((8, cols), F32)],
        [SMEM] + [VMEM] * (2 * swaps) + [ANY, ANY],
        scratch=[
            pltpu.VMEM(square, scratch_type),
            pltpu.VMEM(square, F32),
            pltpu.VMEM(square, F32),
            pltpu.SemaphoreType.DMA,
        ],
        flops=1,
        vmem=20,
    )(book, *mine, *other, left_stats, right_other)
    root = fence([root], *rests_met)[0]
    root_other = exchange(root, "fsdp", 1, indices)

    def finish_body(mine_ref, other_ref, graft_ref, *refs):
        out_refs, result = refs[:planes], refs[planes]
        _, plane_here, core_here = place()
        left_here = jnp.sum(graft_ref[1:2, :]) > 0.5

        @pl.when(left_here)
        def _():
            result[...] = dot(mine_ref[...], other_ref[...])

        @pl.when(jnp.logical_not(left_here))
        def _():
            result[...] = dot(other_ref[...], mine_ref[...])

        value = result[...]
        mean = jnp.sum(value * value) / entries
        graft_mean = jnp.sum(graft_ref[0:1, :]) / entries
        scale = jnp.sqrt(graft_mean) / jnp.sqrt(mean + 1e-06)
        for k in range(planes):
            row = pl.multiple_of((2 * (plane_here ^ k) + core_here) * rows, rows)
            out_refs[k][...] = (result[pl.ds(row, rows), :] * scale).astype(BF16)

    slabs = call(
        finish_body,
        [shape((rows, order), BF16)] * planes,
        [VMEM, VMEM, VMEM],
        scratch=[pltpu.VMEM(square, F32)],
        flops=2 * order**3,
    )(root, root_other, graft_sum)

    def side_body(slot_ref, whole_ref, *refs):
        met_refs, rest_refs = refs[: reps - 1], refs[reps - 1 : 2 * reps - 2]
        keep_ref, give_ref, held = refs[2 * reps - 2 :]
        rep_here, _, core_here = place()
        local = slot_ref[0, at_local + rep_here]
        for s in range(per):
            held[0, s] = whole_ref[s * piece_rows : (s + 1) * piece_rows, :]
        for j in rep_partners:
            held[j, local] = met_refs[j - 1][:piece_rows, :]
            for i in range(per - 1):
                held[j, (local + 1 + i) % per] = rest_refs[j - 1][
                    i * piece_rows : (i + 1) * piece_rows, :
                ]
        for j in range(reps):
            for m in range(most):
                keep_ref[j, m] = held[j, core_here * most + m]
                give_ref[j, m] = held[j, (1 - core_here) * most + m]

    side = shape((reps, most, piece_rows, cols), BF16)
    keep, give = call(
        side_body,
        [side, side],
        [SMEM] + [VMEM] * (2 * reps - 1),
        scratch=[pltpu.VMEM((reps, per, piece_rows, cols), BF16)],
    )(book, whole, *met[1:], *rests_met)
    other_side = exchange(give, "fsdp", 1, indices)

    returned = [slabs[0]] + [
        exchange(slabs[k], "fsdp", 2 * k, indices) for k in plane_partners
    ]

    share_lasts = [
        exchange(
            fence([jnp.concatenate([shares[m], share_firsts[m]])], slabs[0])[0],
            "rep",
            ways[m][1],
            reps,
        )
        for m in range(2)
    ]

    def stats_body(left_ref, right_ref, after_ref, keep_ref, other_ref,
                   left_out, right_out, token_ref, grad):
        m = pl.program_id(0)
        token_ref[...] = jnp.zeros_like(token_ref)
        rep_here, plane_here, core_here = place()
        for j in range(reps):
            for ref, side in ((keep_ref, core_here), (other_ref, 1 - core_here)):
                for k in range(planes):
                    assemble(grad, rep_here, plane_here, side,
                             ref[j, m, k * rows : (k + 1) * rows, :], k, j)
        value = grad[...].astype(BF16)
        left_out[0] = left_ref[0] + gram(value, 1)
        right_out[0] = right_ref[0] + gram(value, 0)

    token = shape((8, 128), F32)
    slot_block = pl.BlockSpec((1, order, order), lambda m: (m, 0, 0))
    left_new, right_new, stats_token = pl.pallas_call(
        stats_body,
        grid=(most,),
        out_shape=[shape(left_stats.shape, F32), shape(right_stats.shape, F32), token],
        in_specs=[slot_block, slot_block, ANY, VMEM, VMEM],
        out_specs=[slot_block, slot_block, pl.BlockSpec((8, 128), lambda m: (0, 0))],
        scratch_shapes=[pltpu.VMEM(square, scratch_type)],
        compiler_params=pltpu.CompilerParams(vmem_limit_bytes=20 * MIB),
        cost_estimate=pl.CostEstimate(
            flops=1, bytes_accessed=1, transcendentals=0
        ),
    )(left_stats, right_stats, slabs[0], keep, other_side)

    def pick_body(slot_ref, *refs):
        out_ref = refs[-1]
        for k in range(planes):
            spot = slot_ref[0, at_place + k]

            @pl.when(spot >= 0)
            def _():
                out_ref[spot] = refs[k][...]

    picked = call(
        pick_body,
        shape((share, rows, order), BF16),
        [SMEM] + [VMEM] * planes + [ANY],
    )(book, *returned, stats_token)
    picked = fence(fence([picked], flops=LONG), *share_lasts)[0]
    gathered = [picked] + [exchange(picked, "rep", j, reps) for j in rep_partners]

    def accum_body(accum_ref, vocab_ref, after_ref, *refs):

        def piece(j, first, count):
            m, at = first // share_rows, first % share_rows
            near, far = ways[m]
            ref, base = {
                0: (refs[m], 0),
                near: (refs[2 + m], 0),
                far: (refs[4 + m], 0),
                near ^ far: (refs[4 + m], share_rows),
            }[j]
            return ref[base + at : base + at + count, :].astype(F32)

        accum_out, vocab_out, step_out, token_ref = refs[6:]
        token_ref[...] = jnp.zeros_like(token_ref)
        rep_here = place()[0]
        for j in range(reps):
            at = pl.ds(pl.multiple_of((rep_here ^ j) * cols, cols), cols)
            for b in range(blocks):
                value = piece(j, b * rows, rows)
                accum_out[b, :, at] = accum_ref[b, :, at] + value * value
            for i in range(chunks):
                value = piece(j, grad_rows + i * pair_rows, pair_rows)
                value = value.reshape(vocab_own.shape[:2] + (cols,))
                start = pl.multiple_of((rep_here ^ j) * vocab_cols + i * cols, cols)
                at_vocab = pl.ds(start, cols)
                accum = vocab_ref[:, :, at_vocab] + value * value
                vocab_out[:, :, at_vocab] = accum
                step_out[:, :, at_vocab] = (value / (jnp.sqrt(accum) + 1e-10)).astype(BF16)

    graft_accum_new, vocab_accum_new, vocab_step, accum_token = call(
        accum_body,
        [
            shape(graft_accum.shape, F32),
            shape(vocab_accum.shape, F32),
            shape(vocab_accum.shape, BF16),
            token,
        ],
        [VMEM, VMEM, ANY] + [VMEM] * 6,
        vmem=12,
    )(graft_accum, vocab_accum, picked, *shares, *share_firsts, *share_lasts)

    def place_body(slot_ref, *refs):
        out_ref, sem = refs[reps + 1 :]
        rep_here = place()[0]

        copies = []
        for j in range(reps):
            for m in range(share):
                block = slot_ref[0, at_block + m * reps + (rep_here ^ j)]
                copies.append(
                    pltpu.make_async_copy(
                        refs[j].at[m], out_ref.at[block], sem.at[j * share + m]
                    )
                )
                copies[-1].start()
        for copy in copies:
            copy.wait()

    direction = call(
        place_body,
        shape((blocks, rows, order), BF16),
        [SMEM] + [VMEM] * reps + [ANY],
        out_specs=HBM,
        scratch=[pltpu.SemaphoreType.DMA((blocks,))],
    )(book, *gathered, accum_token)
    return (direction, graft_accum_new, left_new, right_new, vocab_accum_new, vocab_step)


def solution(mesh):
    in_specs = (
        P("rep", None, "fsdp", None),
        P(None, "fsdp", None),
        P("fsdp", None, None),
        P("fsdp", None, None),
        P(),
        P("rep", None, "fsdp", None),
        P(None, "fsdp", None),
    )
    out_specs = (
        P(None, "fsdp", None),
        P(None, "fsdp", None),
        P("fsdp", None, None),
        P("fsdp", None, None),
        P(None, "fsdp", None),
        P(None, "fsdp", None),
    )
    return jax.shard_map(
        on_device, mesh=mesh, in_specs=in_specs, out_specs=out_specs, check_vma=False
    )
```

```python
import jax
import jax.numpy as jnp
from jax import lax
from jax.experimental import pallas as pl
from jax.experimental.pallas import tpu as pltpu
from jax.sharding import PartitionSpec as P

ITERS = 6
TAIL = 16
F32 = jnp.float32
BF16 = jnp.bfloat16
VMEM = pl.BlockSpec(memory_space=pltpu.VMEM)
SMEM = pl.BlockSpec(memory_space=pltpu.SMEM)
ANY = pl.BlockSpec(memory_space=pl.ANY)
HBM = pl.BlockSpec(memory_space=pltpu.HBM)
MIB = 1 << 20
LONG = 4 * 10**9
SWAP = 1


def shape(dims, dtype):
    return jax.ShapeDtypeStruct(dims, dtype)


def call(body, outs, in_specs, out_specs=None, scratch=(), flops=1, vmem=8):
    return pl.pallas_call(
        body,
        out_shape=outs,
        in_specs=in_specs,
        out_specs=jax.tree.map(lambda _: VMEM, outs) if out_specs is None else out_specs,
        scratch_shapes=list(scratch),
        compiler_params=pltpu.CompilerParams(vmem_limit_bytes=vmem * MIB),
        cost_estimate=pl.CostEstimate(flops=flops, bytes_accessed=1, transcendentals=0),
    )


def dot(left, right, left_axis=1, right_axis=0):
    return lax.dot_general(
        left, right, (((left_axis,), (right_axis,)), ((), ())), preferred_element_type=F32
    )


def gram(value, axis):
    return dot(value, value, axis, axis)


def three_terms(value):
    high = value.astype(BF16).astype(F32)
    middle = (value - high).astype(BF16).astype(F32)
    return high, middle, value - high - middle


def exchange(values, axis, mask, size):
    return lax.ppermute(values, axis, [(i, i ^ mask) for i in range(size)])


def fence(arrays, *done, flops=1):
    def body(*refs):
        pass

    return pl.pallas_call(
        body,
        out_shape=[shape(array.shape, array.dtype) for array in arrays],
        in_specs=[ANY] * (len(arrays) + len(done)),
        out_specs=[ANY] * len(arrays),
        input_output_aliases={i: i for i in range(len(arrays))},
        compiler_params=pltpu.CompilerParams(vmem_limit_bytes=MIB),
        cost_estimate=pl.CostEstimate(flops=flops, bytes_accessed=1, transcendentals=0),
    )(*arrays, *done)


def late(arrays, *done):
    return fence(fence(arrays, flops=LONG), *done)


def in_hbm(array):
    return pltpu.with_memory_space_constraint(array, pltpu.HBM)


def place():
    index = lax.axis_index("fsdp")
    return lax.axis_index("rep"), index // 2, index % 2


def on_device(
    grad_blocks, graft_accum, left_stats, right_stats, block_slot, vocab_grads, vocab_accum
):
    reps, indices = lax.axis_size("rep"), lax.axis_size("fsdp")
    blocks, rows, order = grad_blocks.shape[1:]
    most = left_stats.shape[0]
    planes, per, cols = indices // 2, 2 * most, order // reps
    assert per <= reps and blocks % reps == 0
    share, slots = blocks // reps, per * planes
    rep_partners, plane_partners = range(1, reps), range(1, planes)
    entries = float(order * order)
    square = (order, order)
    scratch_type = BF16 if rows % 16 == 0 else F32
    vocab_own = vocab_grads[0]
    vocab_cols = vocab_own.shape[2] // reps
    grad_rows, pair_rows = blocks * rows, vocab_own.shape[0] * vocab_own.shape[1]
    chunks = vocab_cols // cols
    vocab_rows = chunks * pair_rows
    share_rows = (grad_rows + vocab_rows) // 2
    assert share_rows % rows == 0 and share_rows % pair_rows == 0
    assert reps == 4 and most == 2
    ways = ((1, 2), (2, 1))
    right_other = exchange(right_stats, "fsdp", 1, indices)

    def ranked(slot_ref, who, visit):
        for s in range(slots):
            who[s] = -1
        for b in range(blocks):
            who[slot_ref[0, b]] = b
        count = jnp.int32(0)
        for s in range(slots):
            block = who[s]
            visit(s, block, count)
            count = count + jnp.where(block >= 0, 1, 0)

    at_local, at_place, at_block = 0, reps, reps + planes
    width = -(-(at_block + blocks) // 128) * 128

    def book_body(slot_ref, out_ref, who):
        rep_here, plane_here, _ = place()
        line = lax.broadcasted_iota(jnp.int32, out_ref.shape, 1)
        out_ref[...] = jnp.where((line >= at_place) & (line < at_block), -1, 0)

        def visit(s, block, count):
            @pl.when(block >= 0)
            def _():
                entry = out_ref[...]
                here = (plane_here == s // per) & (line == at_local + count % reps)
                entry = jnp.where(here, s % per, entry)
                near = (count % reps == rep_here) & (
                    line == at_place + (plane_here ^ (s // per))
                )
                entry = jnp.where(near, count // reps, entry)
                out_ref[...] = jnp.where(line == at_block + count, block, entry)

        ranked(slot_ref, who, visit)

    def cut_body(slot_ref, grad_ref, vocab_ref, *refs):
        out_refs, table_ref = refs[:reps], refs[reps]
        line = lax.broadcasted_iota(jnp.int32, table_ref.shape, 1)
        table = jnp.zeros(table_ref.shape, jnp.int32)
        for b in range(blocks):
            table = jnp.where(line == b, slot_ref[b], table)
        table_ref[...] = table
        for k in range(reps):
            part = place()[0] ^ k
            at = pl.ds(pl.multiple_of(part * cols, cols), cols)
            for b in range(blocks):
                out_refs[k][b * rows : (b + 1) * rows, :] = grad_ref[b, :, at]
            at = pl.ds(pl.multiple_of(part * vocab_cols, vocab_cols), vocab_cols)
            value = vocab_ref[:, :, at].astype(F32).reshape(pair_rows, vocab_cols).astype(BF16)
            for i in range(chunks):
                first = grad_rows + i * pair_rows
                out_refs[k][first : first + pair_rows, :] = value[:, i * cols : (i + 1) * cols]

    cut = call(
        cut_body,
        [shape((grad_rows + vocab_rows, cols), BF16)] * reps
        + [shape((1, 128), jnp.int32)],
        [SMEM, VMEM, VMEM],
        vmem=8,
    )(in_hbm(block_slot), in_hbm(grad_blocks[0]), in_hbm(vocab_own))
    pieces, table = cut[:reps], cut[reps]
    accum_share = lax.dynamic_slice_in_dim(
        graft_accum, lax.axis_index("rep") * cols, cols, 2
    )

    terms = [pieces[0]] + [exchange(pieces[k], "rep", k, reps) for k in rep_partners]
    payload_rows = per * rows + TAIL

    book = call(
        book_body,
        shape((1, width), jnp.int32),
        [SMEM],
        scratch=[pltpu.SMEM((slots,), jnp.int32)],
    )(table)

    def sum_body(slot_ref, *refs):
        term_refs, accum_ref, share_refs = refs[:reps], refs[reps], refs[reps + 1 : reps + 3]
        out_refs = refs[reps + 3 : reps + 3 + planes]
        held, parts, tail = refs[reps + 3 + planes :]
        plane_here = place()[1]

        def total_of(first, count):
            total = term_refs[0][first : first + count, :].astype(F32)
            for term in term_refs[1:]:
                total = total + term[first : first + count, :].astype(F32)
            return total.astype(BF16)

        def keep(first, value):
            half, at = first // share_rows, first % share_rows
            share_refs[half][at : at + value.shape[0], :] = value

        for i in range(chunks):
            first = grad_rows + i * pair_rows
            keep(first, total_of(first, pair_rows))
        held[...] = jnp.zeros_like(held)
        parts[...] = jnp.zeros_like(parts)
        for b in range(blocks):
            summed = total_of(b * rows, rows)
            keep(b * rows, summed)
            value = summed.astype(F32)
            grafted = value / (jnp.sqrt(accum_ref[b] + value * value) + 1e-10)
            slot = slot_ref[0, b]
            away = (slot // per) ^ plane_here
            local = slot % per
            held[away, local] = summed
            parts[away, pl.ds(local, 1), :] = jnp.sum(grafted * grafted, axis=0, keepdims=True)
        tail[...] = jnp.zeros_like(tail)
        for k in range(planes):
            for s in range(per):
                out_refs[k][s * rows : (s + 1) * rows, :] = held[k, s]
            for t, term in enumerate(three_terms(parts[k, :per, :])):
                tail[t * per : (t + 1) * per, :] = term
            out_refs[k][per * rows :, :] = tail[...].astype(BF16)

    summed = call(
        sum_body,
        [shape((share_rows, cols), BF16)] * 2
        + [shape((payload_rows, cols), BF16)] * planes,
        [SMEM] + [VMEM] * (reps + 1),
        scratch=[
            pltpu.VMEM((planes, per, rows, cols), BF16),
            pltpu.VMEM((planes, 8, cols), F32),
            pltpu.VMEM((TAIL, cols), F32),
        ],
    )(table, *terms, accum_share)
    shares, payloads = summed[:2], summed[2:]

    arrived = [payloads[0]] + [
        exchange(payloads[k], "fsdp", 2 * k, indices) for k in plane_partners
    ]

    share_firsts = [exchange(shares[m], "rep", ways[m][0], reps) for m in range(2)]
    part_rows = planes * rows + TAIL

    def route_body(slot_ref, *refs):
        in_refs = refs[:planes]
        out_refs = refs[planes : planes + reps]
        whole_ref, rest_refs = refs[planes + reps], refs[planes + reps + 1 : planes + 2 * reps]
        parts, tail = refs[planes + 2 * reps :]
        rep_here = place()[0]
        total = jnp.zeros((per, cols), F32)
        for ref in in_refs:
            bits = ref[per * rows :, :].astype(F32)
            for t in range(3):
                total = total + bits[t * per : (t + 1) * per]
        parts[:per, :] = total
        tail[...] = jnp.zeros_like(tail)
        for j in range(reps):
            local = slot_ref[0, at_local + (rep_here ^ j)]
            for s in range(per):

                @pl.when(local == s)
                def _():
                    for k in range(planes):
                        out_refs[j][k * rows : (k + 1) * rows, :] = in_refs[k][
                            s * rows : (s + 1) * rows, :
                        ]

            for t, term in enumerate(three_terms(parts[pl.ds(local, 1), :])):
                tail[t : t + 1, :] = term
            out_refs[j][planes * rows :, :] = tail[...].astype(BF16)
        piece = planes * rows
        for k in range(planes):
            for s in range(per):
                at = s * piece + k * rows
                whole_ref[at : at + rows, :] = in_refs[k][s * rows : (s + 1) * rows, :]
        for j in rep_partners:
            for i in range(per - 1):
                first = (slot_ref[0, at_local + (rep_here ^ j)] + 1 + i) % per * piece
                rest_refs[j - 1][i * piece : (i + 1) * piece, :] = whole_ref[
                    pl.ds(pl.multiple_of(first, piece), piece), :
                ]

    piece_rows = planes * rows
    routed = call(
        route_body,
        [shape((part_rows, cols), BF16)] * reps
        + [shape((per * piece_rows, cols), BF16)]
        + [shape(((per - 1) * piece_rows, cols), BF16)] * (reps - 1),
        [SMEM] + [VMEM] * planes,
        scratch=[pltpu.VMEM((8, cols), F32), pltpu.VMEM((TAIL, cols), F32)],
    )(book, *arrived)
    routed = late(routed, *share_firsts, right_other)
    parts, whole, rests = routed[:reps], routed[reps], routed[reps + 1 :]

    met = [parts[0]] + [exchange(parts[j], "rep", j, reps) for j in rep_partners]
    mine = [jnp.stack(met[i : i + SWAP]) for i in range(0, reps, SWAP)]
    other = [exchange(array, "fsdp", 1, indices) for array in mine]

    rests_met = [exchange(rests[j - 1], "rep", j, reps) for j in rep_partners]

    def assemble(grad, rep_here, plane_here, core_here, piece, k, j):
        row = pl.multiple_of((2 * (plane_here ^ k) + core_here) * rows, rows)
        col = pl.multiple_of((rep_here ^ j) * cols, cols)
        grad[pl.ds(row, rows), pl.ds(col, cols)] = piece.astype(scratch_type)

    swaps, side = len(mine), order // 2

    def root_body(slot_ref, *refs):
        mine_refs, other_refs = refs[:swaps], refs[swaps : 2 * swaps]
        left_ref, right_ref, out_ref, graft_ref, grad, matrix, start, sem = refs[2 * swaps :]
        rep_here, plane_here, core_here = place()
        local = slot_ref[0, at_local + rep_here]
        owner, at = local // most, local % most

        @pl.when(owner == core_here)
        def _():
            pltpu.make_async_copy(left_ref.at[at], matrix, sem).start()

        @pl.when(owner != core_here)
        def _():
            pltpu.make_async_copy(right_ref.at[at], matrix, sem).start()

        graft = jnp.zeros((1, cols), F32)
        for j in range(reps):
            for swap_refs, which in ((mine_refs, core_here), (other_refs, 1 - core_here)):
                ref = swap_refs[j // SWAP].at[j % SWAP]
                for k in range(planes):
                    assemble(grad, rep_here, plane_here, which,
                             ref[k * rows : (k + 1) * rows, :], k, j)
                bits = ref[planes * rows :, :].astype(F32)
                graft = graft + jnp.sum(bits[:8], axis=0, keepdims=True)
        line = lax.broadcasted_iota(jnp.int32, graft_ref.shape, 0)
        first = jnp.where(owner == core_here, 1.0, 0.0)
        graft_ref[...] = jnp.where(line == 0, jnp.broadcast_to(graft, graft_ref.shape), first)
        pltpu.make_async_copy(left_ref.at[at], matrix, sem).wait()

        @pl.when(owner == core_here)
        def _():
            value = grad[...].astype(BF16)
            matrix[:side, :] += dot(value[:side], value, 1, 1)
            matrix[side:, side:] += gram(value[side:], 1)
            start[...] = value.astype(F32)

        @pl.when(owner != core_here)
        def _():
            value = grad[...].astype(BF16)
            matrix[:side, :] += dot(value[:, :side], value, 0, 0)
            matrix[side:, side:] += gram(value[:, side:], 0)
            line = lax.broadcasted_iota(jnp.int32, square, 0)
            start[...] = (line == lax.broadcasted_iota(jnp.int32, square, 1)).astype(F32)

        upper, corner = matrix[:side, :], matrix[side:, side:]
        total = jnp.sum(upper[:, :side] * upper[:, :side]) + jnp.sum(corner * corner)
        total = total + 2.0 * jnp.sum(upper[:, side:] * upper[:, side:])
        upper, corner = upper / jnp.sqrt(total), corner / jnp.sqrt(total)
        result = start[...]

        def lower(top, last):
            return jnp.concatenate([top[:, side:].T, last], axis=1)

        for iteration in range(ITERS):
            top = upper.astype(BF16)
            bottom = lower(top, corner.astype(BF16))
            low = jnp.concatenate([top, bottom], axis=0)
            result = 1.25 * result - 0.25 * dot(low, result.astype(BF16))
            if iteration + 1 < ITERS:
                step_top = (dot(top, low) * 0.0625 - 0.625 * upper).astype(BF16)
                step_last = dot(bottom, low[:, side:]) * 0.0625 - 0.625 * corner
                step = jnp.concatenate(
                    [step_top, lower(step_top, step_last.astype(BF16))], axis=0
                )
                twice_top = 1.5625 * upper + dot(top, step)
                twice_last = 1.5625 * corner + dot(bottom, step[:, side:])
                twice_low = twice_top.astype(BF16)
                upper = 1.5625 * twice_top + dot(twice_low, step)
                corner = 1.5625 * twice_last + dot(
                    lower(twice_low, twice_last.astype(BF16)), step[:, side:]
                )
        out_ref[...] = result.astype(BF16)

    root, graft_sum = call(
        root_body,
        [shape(square, BF16), shape((8, cols), F32)],
        [SMEM] + [VMEM] * (2 * swaps) + [ANY, ANY],
        scratch=[
            pltpu.VMEM(square, scratch_type),
            pltpu.VMEM(square, F32),
            pltpu.VMEM(square, F32),
            pltpu.SemaphoreType.DMA,
        ],
        flops=10**9,
        vmem=20,
    )(book, *mine, *other, left_stats, right_other)
    root = fence([root], *rests_met)[0]
    root_other = exchange(root, "fsdp", 1, indices)

    def finish_body(mine_ref, other_ref, graft_ref, *refs):
        out_refs, result = refs[:planes], refs[planes]
        _, plane_here, core_here = place()
        left_here = jnp.sum(graft_ref[1:2, :]) > 0.5

        @pl.when(left_here)
        def _():
            result[...] = dot(mine_ref[...], other_ref[...])

        @pl.when(jnp.logical_not(left_here))
        def _():
            result[...] = dot(other_ref[...], mine_ref[...])

        value = result[...]
        mean = jnp.sum(value * value) / entries
        graft_mean = jnp.sum(graft_ref[0:1, :]) / entries
        scale = jnp.sqrt(graft_mean) / jnp.sqrt(mean + 1e-06)
        for k in range(planes):
            row = pl.multiple_of((2 * (plane_here ^ k) + core_here) * rows, rows)
            out_refs[k][...] = (result[pl.ds(row, rows), :] * scale).astype(BF16)

    slabs = call(
        finish_body,
        [shape((rows, order), BF16)] * planes,
        [VMEM, VMEM, VMEM],
        scratch=[pltpu.VMEM(square, F32)],
        flops=2 * order**3,
    )(root, root_other, graft_sum)

    def side_body(slot_ref, whole_ref, *refs):
        met_refs, rest_refs = refs[: reps - 1], refs[reps - 1 : 2 * reps - 2]
        keep_ref, give_ref, held = refs[2 * reps - 2 :]
        rep_here, _, core_here = place()
        local = slot_ref[0, at_local + rep_here]
        for s in range(per):
            held[0, s] = whole_ref[s * piece_rows : (s + 1) * piece_rows, :]
        for j in rep_partners:
            held[j, local] = met_refs[j - 1][:piece_rows, :]
            for i in range(per - 1):
                held[j, (local + 1 + i) % per] = rest_refs[j - 1][
                    i * piece_rows : (i + 1) * piece_rows, :
                ]
        for j in range(reps):
            for m in range(most):
                keep_ref[j, m] = held[j, core_here * most + m]
                give_ref[j, m] = held[j, (1 - core_here) * most + m]

    held_shape = shape((reps, most, piece_rows, cols), BF16)
    keep, give = call(
        side_body,
        [held_shape, held_shape],
        [SMEM] + [VMEM] * (2 * reps - 1),
        scratch=[pltpu.VMEM((reps, per, piece_rows, cols), BF16)],
    )(book, whole, *met[1:], *rests_met)
    other_side = exchange(give, "fsdp", 1, indices)

    returned = [slabs[0]] + [
        exchange(slabs[k], "fsdp", 2 * k, indices) for k in plane_partners
    ]

    share_lasts = [
        exchange(
            fence([jnp.concatenate([shares[m], share_firsts[m]])], slabs[0])[0],
            "rep",
            ways[m][1],
            reps,
        )
        for m in range(2)
    ]

    def stats_body(left_ref, right_ref, after_ref, keep_ref, other_ref,
                   left_out, right_out, token_ref, grad):
        m = pl.program_id(0)
        token_ref[...] = jnp.zeros_like(token_ref)
        rep_here, plane_here, core_here = place()
        for j in range(reps):
            for ref, side in ((keep_ref, core_here), (other_ref, 1 - core_here)):
                for k in range(planes):
                    assemble(grad, rep_here, plane_here, side,
                             ref[j, m, k * rows : (k + 1) * rows, :], k, j)
        value = grad[...].astype(BF16)
        left_out[0] = left_ref[0] + gram(value, 1)
        right_out[0] = right_ref[0] + gram(value, 0)

    token = shape((8, 128), F32)
    slot_block = pl.BlockSpec((1, order, order), lambda m: (m, 0, 0))
    left_new, right_new, stats_token = pl.pallas_call(
        stats_body,
        grid=(most,),
        out_shape=[shape(left_stats.shape, F32), shape(right_stats.shape, F32), token],
        in_specs=[slot_block, slot_block, ANY, VMEM, VMEM],
        out_specs=[slot_block, slot_block, pl.BlockSpec((8, 128), lambda m: (0, 0))],
        scratch_shapes=[pltpu.VMEM(square, scratch_type)],
        compiler_params=pltpu.CompilerParams(vmem_limit_bytes=20 * MIB),
        cost_estimate=pl.CostEstimate(
            flops=1, bytes_accessed=1, transcendentals=0
        ),
    )(left_stats, right_stats, slabs[0], keep, other_side)

    def pick_body(slot_ref, *refs):
        out_ref = refs[-1]
        for k in range(planes):
            spot = slot_ref[0, at_place + k]

            @pl.when(spot >= 0)
            def _():
                out_ref[spot] = refs[k][...]

    picked = call(
        pick_body,
        shape((share, rows, order), BF16),
        [SMEM] + [VMEM] * planes + [ANY],
    )(book, *returned, stats_token)
    picked = fence(fence([picked], flops=LONG), *share_lasts)[0]
    gathered = [picked] + [exchange(picked, "rep", j, reps) for j in rep_partners]

    def accum_body(accum_ref, vocab_ref, after_ref, *refs):

        def piece(j, first, count):
            m, at = first // share_rows, first % share_rows
            near, far = ways[m]
            ref, base = {
                0: (refs[m], 0),
                near: (refs[2 + m], 0),
                far: (refs[4 + m], 0),
                near ^ far: (refs[4 + m], share_rows),
            }[j]
            return ref[base + at : base + at + count, :].astype(F32)

        accum_out, vocab_out, step_out, token_ref = refs[6:]
        token_ref[...] = jnp.zeros_like(token_ref)
        rep_here = place()[0]
        for j in range(reps):
            at = pl.ds(pl.multiple_of((rep_here ^ j) * cols, cols), cols)
            for b in range(blocks):
                value = piece(j, b * rows, rows)
                accum_out[b, :, at] = accum_ref[b, :, at] + value * value
            for i in range(chunks):
                value = piece(j, grad_rows + i * pair_rows, pair_rows)
                value = value.reshape(vocab_own.shape[:2] + (cols,))
                start = pl.multiple_of((rep_here ^ j) * vocab_cols + i * cols, cols)
                at_vocab = pl.ds(start, cols)
                accum = vocab_ref[:, :, at_vocab] + value * value
                vocab_out[:, :, at_vocab] = accum
                step_out[:, :, at_vocab] = (value / (jnp.sqrt(accum) + 1e-10)).astype(BF16)

    graft_accum_new, vocab_accum_new, vocab_step, accum_token = call(
        accum_body,
        [
            shape(graft_accum.shape, F32),
            shape(vocab_accum.shape, F32),
            shape(vocab_accum.shape, BF16),
            token,
        ],
        [VMEM, VMEM, ANY] + [VMEM] * 6,
        vmem=12,
    )(graft_accum, vocab_accum, picked, *shares, *share_firsts, *share_lasts)

    def place_body(slot_ref, *refs):
        out_ref, sem = refs[reps + 1 :]
        rep_here = place()[0]

        copies = []
        for j in range(reps):
            for m in range(share):
                block = slot_ref[0, at_block + m * reps + (rep_here ^ j)]
                copies.append(
                    pltpu.make_async_copy(
                        refs[j].at[m], out_ref.at[block], sem.at[j * share + m]
                    )
                )
                copies[-1].start()
        for copy in copies:
            copy.wait()

    direction = call(
        place_body,
        shape((blocks, rows, order), BF16),
        [SMEM] + [VMEM] * reps + [ANY],
        out_specs=HBM,
        scratch=[pltpu.SemaphoreType.DMA((blocks,))],
    )(book, *gathered, accum_token)
    return (direction, graft_accum_new, left_new, right_new, vocab_accum_new, vocab_step)


def solution(mesh):
    in_specs = (
        P("rep", None, "fsdp", None),
        P(None, "fsdp", None),
        P("fsdp", None, None),
        P("fsdp", None, None),
        P(),
        P("rep", None, "fsdp", None),
        P(None, "fsdp", None),
    )
    out_specs = (
        P(None, "fsdp", None),
        P(None, "fsdp", None),
        P("fsdp", None, None),
        P("fsdp", None, None),
        P(None, "fsdp", None),
        P(None, "fsdp", None),
    )
    return jax.shard_map(
        on_device, mesh=mesh, in_specs=in_specs, out_specs=out_specs, check_vma=False
    )
```

```python
import jax
import jax.numpy as jnp
from jax import lax
from jax.experimental import pallas as pl
from jax.experimental.pallas import tpu as pltpu
from jax.sharding import PartitionSpec as P

ITERS = 6
TAIL = 16
F32 = jnp.float32
BF16 = jnp.bfloat16
VMEM = pl.BlockSpec(memory_space=pltpu.VMEM)
SMEM = pl.BlockSpec(memory_space=pltpu.SMEM)
ANY = pl.BlockSpec(memory_space=pl.ANY)
HBM = pl.BlockSpec(memory_space=pltpu.HBM)
MIB = 1 << 20
LONG = 4 * 10**9
SWAP = 1


def shape(dims, dtype):
    return jax.ShapeDtypeStruct(dims, dtype)


def call(body, outs, in_specs, out_specs=None, scratch=(), flops=1, vmem=8):
    return pl.pallas_call(
        body,
        out_shape=outs,
        in_specs=in_specs,
        out_specs=jax.tree.map(lambda _: VMEM, outs) if out_specs is None else out_specs,
        scratch_shapes=list(scratch),
        compiler_params=pltpu.CompilerParams(vmem_limit_bytes=vmem * MIB),
        cost_estimate=pl.CostEstimate(flops=flops, bytes_accessed=1, transcendentals=0),
    )


def dot(left, right, left_axis=1, right_axis=0):
    return lax.dot_general(
        left, right, (((left_axis,), (right_axis,)), ((), ())), preferred_element_type=F32
    )


def gram(value, axis):
    return dot(value, value, axis, axis)


def three_terms(value):
    high = value.astype(BF16).astype(F32)
    middle = (value - high).astype(BF16).astype(F32)
    return high, middle, value - high - middle


def exchange(values, axis, mask, size):
    return lax.ppermute(values, axis, [(i, i ^ mask) for i in range(size)])


def fence(arrays, *done, flops=1):
    def body(*refs):
        pass

    return pl.pallas_call(
        body,
        out_shape=[shape(array.shape, array.dtype) for array in arrays],
        in_specs=[ANY] * (len(arrays) + len(done)),
        out_specs=[ANY] * len(arrays),
        input_output_aliases={i: i for i in range(len(arrays))},
        compiler_params=pltpu.CompilerParams(vmem_limit_bytes=MIB),
        cost_estimate=pl.CostEstimate(flops=flops, bytes_accessed=1, transcendentals=0),
    )(*arrays, *done)


def late(arrays, *done):
    return fence(fence(arrays, flops=LONG), *done)


def in_hbm(array):
    return pltpu.with_memory_space_constraint(array, pltpu.HBM)


def place():
    index = lax.axis_index("fsdp")
    return lax.axis_index("rep"), index // 2, index % 2


def on_device(
    grad_blocks, graft_accum, left_stats, right_stats, block_slot, vocab_grads, vocab_accum
):
    reps, indices = lax.axis_size("rep"), lax.axis_size("fsdp")
    blocks, rows, order = grad_blocks.shape[1:]
    most = left_stats.shape[0]
    planes, per, cols = indices // 2, 2 * most, order // reps
    assert per <= reps and blocks % reps == 0
    share, slots = blocks // reps, per * planes
    rep_partners, plane_partners = range(1, reps), range(1, planes)
    entries = float(order * order)
    square = (order, order)
    scratch_type = BF16 if rows % 16 == 0 else F32
    vocab_own = vocab_grads[0]
    vocab_cols = vocab_own.shape[2] // reps
    grad_rows, pair_rows = blocks * rows, vocab_own.shape[0] * vocab_own.shape[1]
    chunks = vocab_cols // cols
    vocab_rows = chunks * pair_rows
    share_rows = (grad_rows + vocab_rows) // 2
    assert share_rows % rows == 0 and share_rows % pair_rows == 0
    assert reps == 4 and most == 2
    ways = ((1, 2), (2, 1))
    right_other = exchange(right_stats, "fsdp", 1, indices)

    def ranked(slot_ref, who, visit):
        for s in range(slots):
            who[s] = -1
        for b in range(blocks):
            who[slot_ref[0, b]] = b
        count = jnp.int32(0)
        for s in range(slots):
            block = who[s]
            visit(s, block, count)
            count = count + jnp.where(block >= 0, 1, 0)

    at_local, at_place, at_block = 0, reps, reps + planes
    width = -(-(at_block + blocks) // 128) * 128

    def book_body(slot_ref, out_ref, who):
        rep_here, plane_here, _ = place()
        line = lax.broadcasted_iota(jnp.int32, out_ref.shape, 1)
        out_ref[...] = jnp.where((line >= at_place) & (line < at_block), -1, 0)

        def visit(s, block, count):
            @pl.when(block >= 0)
            def _():
                entry = out_ref[...]
                here = (plane_here == s // per) & (line == at_local + count % reps)
                entry = jnp.where(here, s % per, entry)
                near = (count % reps == rep_here) & (
                    line == at_place + (plane_here ^ (s // per))
                )
                entry = jnp.where(near, count // reps, entry)
                out_ref[...] = jnp.where(line == at_block + count, block, entry)

        ranked(slot_ref, who, visit)

    def cut_body(slot_ref, grad_ref, vocab_ref, *refs):
        out_refs, table_ref = refs[:reps], refs[reps]
        line = lax.broadcasted_iota(jnp.int32, table_ref.shape, 1)
        table = jnp.zeros(table_ref.shape, jnp.int32)
        for b in range(blocks):
            table = jnp.where(line == b, slot_ref[b], table)
        table_ref[...] = table
        for k in range(reps):
            part = place()[0] ^ k
            at = pl.ds(pl.multiple_of(part * cols, cols), cols)
            for b in range(blocks):
                out_refs[k][b * rows : (b + 1) * rows, :] = grad_ref[b, :, at]
            at = pl.ds(pl.multiple_of(part * vocab_cols, vocab_cols), vocab_cols)
            value = vocab_ref[:, :, at].astype(F32).reshape(pair_rows, vocab_cols).astype(BF16)
            for i in range(chunks):
                first = grad_rows + i * pair_rows
                out_refs[k][first : first + pair_rows, :] = value[:, i * cols : (i + 1) * cols]

    cut = call(
        cut_body,
        [shape((grad_rows + vocab_rows, cols), BF16)] * reps
        + [shape((1, 128), jnp.int32)],
        [SMEM, VMEM, VMEM],
        vmem=8,
    )(in_hbm(block_slot), in_hbm(grad_blocks[0]), in_hbm(vocab_own))
    pieces, table = cut[:reps], cut[reps]
    accum_share = lax.dynamic_slice_in_dim(
        graft_accum, lax.axis_index("rep") * cols, cols, 2
    )

    terms = [pieces[0]] + [exchange(pieces[k], "rep", k, reps) for k in rep_partners]
    payload_rows = per * rows + TAIL

    book = call(
        book_body,
        shape((1, width), jnp.int32),
        [SMEM],
        scratch=[pltpu.SMEM((slots,), jnp.int32)],
    )(table)

    def sum_body(slot_ref, *refs):
        term_refs, accum_ref, share_refs = refs[:reps], refs[reps], refs[reps + 1 : reps + 3]
        out_refs = refs[reps + 3 : reps + 3 + planes]
        held, parts, tail = refs[reps + 3 + planes :]
        plane_here = place()[1]

        def total_of(first, count):
            total = term_refs[0][first : first + count, :].astype(F32)
            for term in term_refs[1:]:
                total = total + term[first : first + count, :].astype(F32)
            return total.astype(BF16)

        def keep(first, value):
            half, at = first // share_rows, first % share_rows
            share_refs[half][at : at + value.shape[0], :] = value

        for i in range(chunks):
            first = grad_rows + i * pair_rows
            keep(first, total_of(first, pair_rows))
        held[...] = jnp.zeros_like(held)
        parts[...] = jnp.zeros_like(parts)
        for b in range(blocks):
            summed = total_of(b * rows, rows)
            keep(b * rows, summed)
            value = summed.astype(F32)
            grafted = value / (jnp.sqrt(accum_ref[b] + value * value) + 1e-10)
            slot = slot_ref[0, b]
            away = (slot // per) ^ plane_here
            local = slot % per
            held[away, local] = summed
            parts[away, pl.ds(local, 1), :] = jnp.sum(grafted * grafted, axis=0, keepdims=True)
        tail[...] = jnp.zeros_like(tail)
        for k in range(planes):
            for s in range(per):
                out_refs[k][s * rows : (s + 1) * rows, :] = held[k, s]
            for t, term in enumerate(three_terms(parts[k, :per, :])):
                tail[t * per : (t + 1) * per, :] = term
            out_refs[k][per * rows :, :] = tail[...].astype(BF16)

    summed = call(
        sum_body,
        [shape((share_rows, cols), BF16)] * 2
        + [shape((payload_rows, cols), BF16)] * planes,
        [SMEM] + [VMEM] * (reps + 1),
        scratch=[
            pltpu.VMEM((planes, per, rows, cols), BF16),
            pltpu.VMEM((planes, 8, cols), F32),
            pltpu.VMEM((TAIL, cols), F32),
        ],
    )(table, *terms, accum_share)
    shares, payloads = summed[:2], summed[2:]

    arrived = [payloads[0]] + [
        exchange(payloads[k], "fsdp", 2 * k, indices) for k in plane_partners
    ]

    share_firsts = [exchange(shares[m], "rep", ways[m][0], reps) for m in range(2)]
    part_rows = planes * rows + TAIL

    def route_body(slot_ref, *refs):
        in_refs = refs[:planes]
        out_refs = refs[planes : planes + reps]
        whole_ref, rest_refs = refs[planes + reps], refs[planes + reps + 1 : planes + 2 * reps]
        parts, tail = refs[planes + 2 * reps :]
        rep_here = place()[0]
        total = jnp.zeros((per, cols), F32)
        for ref in in_refs:
            bits = ref[per * rows :, :].astype(F32)
            for t in range(3):
                total = total + bits[t * per : (t + 1) * per]
        parts[:per, :] = total
        tail[...] = jnp.zeros_like(tail)
        for j in range(reps):
            local = slot_ref[0, at_local + (rep_here ^ j)]
            for s in range(per):

                @pl.when(local == s)
                def _():
                    for k in range(planes):
                        out_refs[j][k * rows : (k + 1) * rows, :] = in_refs[k][
                            s * rows : (s + 1) * rows, :
                        ]

            for t, term in enumerate(three_terms(parts[pl.ds(local, 1), :])):
                tail[t : t + 1, :] = term
            out_refs[j][planes * rows :, :] = tail[...].astype(BF16)
        piece = planes * rows
        for k in range(planes):
            for s in range(per):
                at = s * piece + k * rows
                whole_ref[at : at + rows, :] = in_refs[k][s * rows : (s + 1) * rows, :]
        for j in rep_partners:
            for i in range(per - 1):
                first = (slot_ref[0, at_local + (rep_here ^ j)] + 1 + i) % per * piece
                rest_refs[j - 1][i * piece : (i + 1) * piece, :] = whole_ref[
                    pl.ds(pl.multiple_of(first, piece), piece), :
                ]

    piece_rows = planes * rows
    routed = call(
        route_body,
        [shape((part_rows, cols), BF16)] * reps
        + [shape((per * piece_rows, cols), BF16)]
        + [shape(((per - 1) * piece_rows, cols), BF16)] * (reps - 1),
        [SMEM] + [VMEM] * planes,
        scratch=[pltpu.VMEM((8, cols), F32), pltpu.VMEM((TAIL, cols), F32)],
    )(book, *arrived)
    routed = late(routed, *share_firsts, right_other)
    parts, whole, rests = routed[:reps], routed[reps], routed[reps + 1 :]

    met = [parts[0]] + [exchange(parts[j], "rep", j, reps) for j in rep_partners]
    mine = [jnp.stack(met[i : i + SWAP]) for i in range(0, reps, SWAP)]
    other = [exchange(array, "fsdp", 1, indices) for array in mine]

    rests_met = [exchange(rests[j - 1], "rep", j, reps) for j in rep_partners]

    def assemble(grad, rep_here, plane_here, core_here, piece, k, j):
        row = pl.multiple_of((2 * (plane_here ^ k) + core_here) * rows, rows)
        col = pl.multiple_of((rep_here ^ j) * cols, cols)
        grad[pl.ds(row, rows), pl.ds(col, cols)] = piece.astype(scratch_type)

    swaps, side = len(mine), order // 2

    def root_body(slot_ref, *refs):
        mine_refs, other_refs = refs[:swaps], refs[swaps : 2 * swaps]
        left_ref, right_ref, out_ref, graft_ref, grad, matrix, start, sem = refs[2 * swaps :]
        rep_here, plane_here, core_here = place()
        local = slot_ref[0, at_local + rep_here]
        owner, at = local // most, local % most

        @pl.when(owner == core_here)
        def _():
            pltpu.make_async_copy(left_ref.at[at], matrix, sem).start()

        @pl.when(owner != core_here)
        def _():
            pltpu.make_async_copy(right_ref.at[at], matrix, sem).start()

        graft = jnp.zeros((1, cols), F32)
        for j in range(reps):
            for swap_refs, which in ((mine_refs, core_here), (other_refs, 1 - core_here)):
                ref = swap_refs[j // SWAP].at[j % SWAP]
                for k in range(planes):
                    assemble(grad, rep_here, plane_here, which,
                             ref[k * rows : (k + 1) * rows, :], k, j)
                bits = ref[planes * rows :, :].astype(F32)
                graft = graft + jnp.sum(bits[:8], axis=0, keepdims=True)
        line = lax.broadcasted_iota(jnp.int32, graft_ref.shape, 0)
        first = jnp.where(owner == core_here, 1.0, 0.0)
        graft_ref[...] = jnp.where(line == 0, jnp.broadcast_to(graft, graft_ref.shape), first)
        pltpu.make_async_copy(left_ref.at[at], matrix, sem).wait()

        @pl.when(owner == core_here)
        def _():
            value = grad[...].astype(BF16)
            matrix[:side, :] += dot(value[:side], value, 1, 1)
            matrix[side:, side:] += gram(value[side:], 1)
            start[...] = value.astype(F32)

        @pl.when(owner != core_here)
        def _():
            value = grad[...].astype(BF16)
            matrix[:side, :] += dot(value[:, :side], value, 0, 0)
            matrix[side:, side:] += gram(value[:, side:], 0)
            line = lax.broadcasted_iota(jnp.int32, square, 0)
            start[...] = (line == lax.broadcasted_iota(jnp.int32, square, 1)).astype(F32)

        upper, corner = matrix[:side, :], matrix[side:, side:]
        total = jnp.sum(upper[:, :side] * upper[:, :side]) + jnp.sum(corner * corner)
        total = total + 2.0 * jnp.sum(upper[:, side:] * upper[:, side:])
        upper, corner = upper / jnp.sqrt(total), corner / jnp.sqrt(total)
        result = start[...]

        def lower(top, last):
            return jnp.concatenate([top[:, side:].T, last], axis=1)

        for iteration in range(ITERS):
            top = upper.astype(BF16)
            bottom = lower(top, corner.astype(BF16))
            low = jnp.concatenate([top, bottom], axis=0)
            result = 1.25 * result - 0.25 * dot(low, result.astype(BF16))
            if iteration + 1 < ITERS:
                step_top = (dot(top, low) * 0.0625 - 0.625 * upper).astype(BF16)
                step_last = dot(bottom, low[:, side:]) * 0.0625 - 0.625 * corner
                step = jnp.concatenate(
                    [step_top, lower(step_top, step_last.astype(BF16))], axis=0
                )
                twice_top = 1.5625 * upper + dot(top, step)
                twice_last = 1.5625 * corner + dot(bottom, step[:, side:])
                twice_low = twice_top.astype(BF16)
                upper = 1.5625 * twice_top + dot(twice_low, step)
                corner = 1.5625 * twice_last + dot(
                    lower(twice_low, twice_last.astype(BF16)), step[:, side:]
                )
        out_ref[...] = result.astype(BF16)

    root, graft_sum = call(
        root_body,
        [shape(square, BF16), shape((8, cols), F32)],
        [SMEM] + [VMEM] * (2 * swaps) + [ANY, ANY],
        scratch=[
            pltpu.VMEM(square, scratch_type),
            pltpu.VMEM(square, F32),
            pltpu.VMEM(square, F32),
            pltpu.SemaphoreType.DMA,
        ],
        flops=10**9,
        vmem=20,
    )(book, *mine, *other, left_stats, right_other)
    root = fence([root], *rests_met)[0]
    root_other = exchange(root, "fsdp", 1, indices)

    def finish_body(mine_ref, other_ref, graft_ref, *refs):
        out_refs, result = refs[:planes], refs[planes]
        _, plane_here, core_here = place()
        left_here = jnp.sum(graft_ref[1:2, :]) > 0.5

        @pl.when(left_here)
        def _():
            result[...] = dot(mine_ref[...], other_ref[...])

        @pl.when(jnp.logical_not(left_here))
        def _():
            result[...] = dot(other_ref[...], mine_ref[...])

        value = result[...]
        mean = jnp.sum(value * value) / entries
        graft_mean = jnp.sum(graft_ref[0:1, :]) / entries
        scale = jnp.sqrt(graft_mean) / jnp.sqrt(mean + 1e-06)
        for k in range(planes):
            row = pl.multiple_of((2 * (plane_here ^ k) + core_here) * rows, rows)
            out_refs[k][...] = (result[pl.ds(row, rows), :] * scale).astype(BF16)

    slabs = call(
        finish_body,
        [shape((rows, order), BF16)] * planes,
        [VMEM, VMEM, VMEM],
        scratch=[pltpu.VMEM(square, F32)],
        flops=2 * order**3,
    )(root, root_other, graft_sum)

    def side_body(slot_ref, whole_ref, *refs):
        met_refs, rest_refs = refs[: reps - 1], refs[reps - 1 : 2 * reps - 2]
        keep_ref, give_ref, held = refs[2 * reps - 2 :]
        rep_here, _, core_here = place()
        local = slot_ref[0, at_local + rep_here]
        for s in range(per):
            held[0, s] = whole_ref[s * piece_rows : (s + 1) * piece_rows, :]
        for j in rep_partners:
            held[j, local] = met_refs[j - 1][:piece_rows, :]
            for i in range(per - 1):
                held[j, (local + 1 + i) % per] = rest_refs[j - 1][
                    i * piece_rows : (i + 1) * piece_rows, :
                ]
        for j in range(reps):
            for m in range(most):
                keep_ref[j, m] = held[j, core_here * most + m]
                give_ref[j, m] = held[j, (1 - core_here) * most + m]

    held_shape = shape((reps, most, piece_rows, cols), BF16)
    keep, give = call(
        side_body,
        [held_shape, held_shape],
        [SMEM] + [VMEM] * (2 * reps - 1),
        scratch=[pltpu.VMEM((reps, per, piece_rows, cols), BF16)],
    )(book, whole, *met[1:], *rests_met)
    other_side = exchange(give, "fsdp", 1, indices)
    slabs = fence(slabs, other_side)

    returned = [slabs[0]] + [
        exchange(slabs[k], "fsdp", 2 * k, indices) for k in plane_partners
    ]

    share_lasts = [
        exchange(
            fence([jnp.concatenate([shares[m], share_firsts[m]])], slabs[0])[0],
            "rep",
            ways[m][1],
            reps,
        )
        for m in range(2)
    ]

    def stats_body(left_ref, right_ref, after_ref, keep_ref, other_ref,
                   left_out, right_out, token_ref, grad):
        m = pl.program_id(0)
        token_ref[...] = jnp.zeros_like(token_ref)
        rep_here, plane_here, core_here = place()
        for j in range(reps):
            for ref, side in ((keep_ref, core_here), (other_ref, 1 - core_here)):
                for k in range(planes):
                    assemble(grad, rep_here, plane_here, side,
                             ref[j, m, k * rows : (k + 1) * rows, :], k, j)
        value = grad[...].astype(BF16)
        left_out[0] = left_ref[0] + gram(value, 1)
        right_out[0] = right_ref[0] + gram(value, 0)

    token = shape((8, 128), F32)
    slot_block = pl.BlockSpec((1, order, order), lambda m: (m, 0, 0))
    left_new, right_new, stats_token = pl.pallas_call(
        stats_body,
        grid=(most,),
        out_shape=[shape(left_stats.shape, F32), shape(right_stats.shape, F32), token],
        in_specs=[slot_block, slot_block, ANY, VMEM, VMEM],
        out_specs=[slot_block, slot_block, pl.BlockSpec((8, 128), lambda m: (0, 0))],
        scratch_shapes=[pltpu.VMEM(square, scratch_type)],
        compiler_params=pltpu.CompilerParams(vmem_limit_bytes=20 * MIB),
        cost_estimate=pl.CostEstimate(
            flops=1, bytes_accessed=1, transcendentals=0
        ),
    )(left_stats, right_stats, slabs[0], keep, other_side)

    def pick_body(slot_ref, *refs):
        out_ref = refs[-1]
        for k in range(planes):
            spot = slot_ref[0, at_place + k]

            @pl.when(spot >= 0)
            def _():
                out_ref[spot] = refs[k][...]

    picked = call(
        pick_body,
        shape((share, rows, order), BF16),
        [SMEM] + [VMEM] * planes + [ANY],
    )(book, *returned, stats_token)
    picked = fence([picked], flops=10**8)[0]
    gathered = [picked] + [exchange(picked, "rep", j, reps) for j in rep_partners]

    def accum_body(accum_ref, vocab_ref, after_ref, *refs):

        def piece(j, first, count):
            m, at = first // share_rows, first % share_rows
            near, far = ways[m]
            ref, base = {
                0: (refs[m], 0),
                near: (refs[2 + m], 0),
                far: (refs[4 + m], 0),
                near ^ far: (refs[4 + m], share_rows),
            }[j]
            return ref[base + at : base + at + count, :].astype(F32)

        accum_out, vocab_out, step_out, token_ref = refs[6:]
        token_ref[...] = jnp.zeros_like(token_ref)
        rep_here = place()[0]
        for j in range(reps):
            at = pl.ds(pl.multiple_of((rep_here ^ j) * cols, cols), cols)
            for b in range(blocks):
                value = piece(j, b * rows, rows)
                accum_out[b, :, at] = accum_ref[b, :, at] + value * value
            for i in range(chunks):
                value = piece(j, grad_rows + i * pair_rows, pair_rows)
                value = value.reshape(vocab_own.shape[:2] + (cols,))
                start = pl.multiple_of((rep_here ^ j) * vocab_cols + i * cols, cols)
                at_vocab = pl.ds(start, cols)
                accum = vocab_ref[:, :, at_vocab] + value * value
                vocab_out[:, :, at_vocab] = accum
                step_out[:, :, at_vocab] = (value / (jnp.sqrt(accum) + 1e-10)).astype(BF16)

    graft_accum_new, vocab_accum_new, vocab_step, accum_token = call(
        accum_body,
        [
            shape(graft_accum.shape, F32),
            shape(vocab_accum.shape, F32),
            shape(vocab_accum.shape, BF16),
            token,
        ],
        [VMEM, VMEM, ANY] + [VMEM] * 6,
        vmem=12,
    )(graft_accum, vocab_accum, picked, *shares, *share_firsts, *share_lasts)

    def place_body(slot_ref, *refs):
        out_ref, sem = refs[reps + 1 :]
        rep_here = place()[0]

        copies = []
        for j in range(reps):
            for m in range(share):
                block = slot_ref[0, at_block + m * reps + (rep_here ^ j)]
                copies.append(
                    pltpu.make_async_copy(
                        refs[j].at[m], out_ref.at[block], sem.at[j * share + m]
                    )
                )
                copies[-1].start()
        for copy in copies:
            copy.wait()

    direction = call(
        place_body,
        shape((blocks, rows, order), BF16),
        [SMEM] + [VMEM] * reps + [ANY],
        out_specs=HBM,
        scratch=[pltpu.SemaphoreType.DMA((blocks,))],
    )(book, *gathered, accum_token)
    return (direction, graft_accum_new, left_new, right_new, vocab_accum_new, vocab_step)


def solution(mesh):
    in_specs = (
        P("rep", None, "fsdp", None),
        P(None, "fsdp", None),
        P("fsdp", None, None),
        P("fsdp", None, None),
        P(),
        P("rep", None, "fsdp", None),
        P(None, "fsdp", None),
    )
    out_specs = (
        P(None, "fsdp", None),
        P(None, "fsdp", None),
        P("fsdp", None, None),
        P("fsdp", None, None),
        P(None, "fsdp", None),
        P(None, "fsdp", None),
    )
    return jax.shard_map(
        on_device, mesh=mesh, in_specs=in_specs, out_specs=out_specs, check_vma=False
    )
```

```python
import jax
import jax.numpy as jnp
from jax import lax
from jax.experimental import pallas as pl
from jax.experimental.pallas import tpu as pltpu
from jax.sharding import PartitionSpec as P

ITERS = 6
TAIL = 16
F32 = jnp.float32
BF16 = jnp.bfloat16
VMEM = pl.BlockSpec(memory_space=pltpu.VMEM)
SMEM = pl.BlockSpec(memory_space=pltpu.SMEM)
ANY = pl.BlockSpec(memory_space=pl.ANY)
HBM = pl.BlockSpec(memory_space=pltpu.HBM)
MIB = 1 << 20
LONG = 4 * 10**9
SWAP = 1


def shape(dims, dtype):
    return jax.ShapeDtypeStruct(dims, dtype)


def call(body, outs, in_specs, out_specs=None, scratch=(), flops=1, vmem=8):
    return pl.pallas_call(
        body,
        out_shape=outs,
        in_specs=in_specs,
        out_specs=jax.tree.map(lambda _: VMEM, outs) if out_specs is None else out_specs,
        scratch_shapes=list(scratch),
        compiler_params=pltpu.CompilerParams(vmem_limit_bytes=vmem * MIB),
        cost_estimate=pl.CostEstimate(flops=flops, bytes_accessed=1, transcendentals=0),
    )


def dot(left, right, left_axis=1, right_axis=0):
    return lax.dot_general(
        left, right, (((left_axis,), (right_axis,)), ((), ())), preferred_element_type=F32
    )


def gram(value, axis):
    return dot(value, value, axis, axis)


def three_terms(value):
    high = value.astype(BF16).astype(F32)
    middle = (value - high).astype(BF16).astype(F32)
    return high, middle, value - high - middle


def exchange(values, axis, mask, size):
    return lax.ppermute(values, axis, [(i, i ^ mask) for i in range(size)])


def fence(arrays, *done, flops=1):
    def body(*refs):
        pass

    return pl.pallas_call(
        body,
        out_shape=[shape(array.shape, array.dtype) for array in arrays],
        in_specs=[ANY] * (len(arrays) + len(done)),
        out_specs=[ANY] * len(arrays),
        input_output_aliases={i: i for i in range(len(arrays))},
        compiler_params=pltpu.CompilerParams(vmem_limit_bytes=MIB),
        cost_estimate=pl.CostEstimate(flops=flops, bytes_accessed=1, transcendentals=0),
    )(*arrays, *done)


def late(arrays, *done):
    return fence(fence(arrays, flops=LONG), *done)


def in_hbm(array):
    return pltpu.with_memory_space_constraint(array, pltpu.HBM)


def place():
    index = lax.axis_index("fsdp")
    return lax.axis_index("rep"), index // 2, index % 2


def on_device(
    grad_blocks, graft_accum, left_stats, right_stats, block_slot, vocab_grads, vocab_accum
):
    reps, indices = lax.axis_size("rep"), lax.axis_size("fsdp")
    blocks, rows, order = grad_blocks.shape[1:]
    most = left_stats.shape[0]
    planes, per, cols = indices // 2, 2 * most, order // reps
    assert per <= reps and blocks % reps == 0
    share, slots = blocks // reps, per * planes
    rep_partners, plane_partners = range(1, reps), range(1, planes)
    entries = float(order * order)
    square = (order, order)
    scratch_type = BF16 if rows % 16 == 0 else F32
    vocab_own = vocab_grads[0]
    vocab_cols = vocab_own.shape[2] // reps
    grad_rows, pair_rows = blocks * rows, vocab_own.shape[0] * vocab_own.shape[1]
    chunks = vocab_cols // cols
    vocab_rows = chunks * pair_rows
    share_rows = (grad_rows + vocab_rows) // 2
    assert share_rows % rows == 0 and share_rows % pair_rows == 0
    assert reps == 4 and most == 2
    ways = ((1, 2), (2, 1))
    right_other = exchange(right_stats, "fsdp", 1, indices)

    def ranked(slot_ref, who, visit):
        for s in range(slots):
            who[s] = -1
        for b in range(blocks):
            who[slot_ref[0, b]] = b
        count = jnp.int32(0)
        for s in range(slots):
            block = who[s]
            visit(s, block, count)
            count = count + jnp.where(block >= 0, 1, 0)

    at_local, at_place, at_block = 0, reps, reps + planes
    width = -(-(at_block + blocks) // 128) * 128

    def book_body(slot_ref, out_ref, who):
        rep_here, plane_here, _ = place()
        line = lax.broadcasted_iota(jnp.int32, out_ref.shape, 1)
        out_ref[...] = jnp.where((line >= at_place) & (line < at_block), -1, 0)

        def visit(s, block, count):
            @pl.when(block >= 0)
            def _():
                entry = out_ref[...]
                here = (plane_here == s // per) & (line == at_local + count % reps)
                entry = jnp.where(here, s % per, entry)
                near = (count % reps == rep_here) & (
                    line == at_place + (plane_here ^ (s // per))
                )
                entry = jnp.where(near, count // reps, entry)
                out_ref[...] = jnp.where(line == at_block + count, block, entry)

        ranked(slot_ref, who, visit)

    def cut_body(slot_ref, grad_ref, vocab_ref, *refs):
        out_refs, table_ref = refs[:reps], refs[reps]
        line = lax.broadcasted_iota(jnp.int32, table_ref.shape, 1)
        table = jnp.zeros(table_ref.shape, jnp.int32)
        for b in range(blocks):
            table = jnp.where(line == b, slot_ref[b], table)
        table_ref[...] = table
        for k in range(reps):
            part = place()[0] ^ k
            at = pl.ds(pl.multiple_of(part * cols, cols), cols)
            for b in range(blocks):
                out_refs[k][b * rows : (b + 1) * rows, :] = grad_ref[b, :, at]
            at = pl.ds(pl.multiple_of(part * vocab_cols, vocab_cols), vocab_cols)
            value = vocab_ref[:, :, at].astype(F32).reshape(pair_rows, vocab_cols).astype(BF16)
            for i in range(chunks):
                first = grad_rows + i * pair_rows
                out_refs[k][first : first + pair_rows, :] = value[:, i * cols : (i + 1) * cols]

    cut = call(
        cut_body,
        [shape((grad_rows + vocab_rows, cols), BF16)] * reps
        + [shape((1, 128), jnp.int32)],
        [SMEM, VMEM, VMEM],
        vmem=8,
    )(in_hbm(block_slot), in_hbm(grad_blocks[0]), in_hbm(vocab_own))
    pieces, table = cut[:reps], cut[reps]
    accum_share = lax.dynamic_slice_in_dim(
        graft_accum, lax.axis_index("rep") * cols, cols, 2
    )

    terms = [pieces[0]] + [exchange(pieces[k], "rep", k, reps) for k in rep_partners]
    payload_rows = per * rows + TAIL

    book = call(
        book_body,
        shape((1, width), jnp.int32),
        [SMEM],
        scratch=[pltpu.SMEM((slots,), jnp.int32)],
    )(table)

    def sum_body(slot_ref, *refs):
        term_refs, accum_ref, share_refs = refs[:reps], refs[reps], refs[reps + 1 : reps + 3]
        out_refs = refs[reps + 3 : reps + 3 + planes]
        held, parts, tail = refs[reps + 3 + planes :]
        plane_here = place()[1]

        def total_of(first, count):
            total = term_refs[0][first : first + count, :].astype(F32)
            for term in term_refs[1:]:
                total = total + term[first : first + count, :].astype(F32)
            return total.astype(BF16)

        def keep(first, value):
            half, at = first // share_rows, first % share_rows
            share_refs[half][at : at + value.shape[0], :] = value

        for i in range(chunks):
            first = grad_rows + i * pair_rows
            keep(first, total_of(first, pair_rows))
        held[...] = jnp.zeros_like(held)
        parts[...] = jnp.zeros_like(parts)
        for b in range(blocks):
            summed = total_of(b * rows, rows)
            keep(b * rows, summed)
            value = summed.astype(F32)
            grafted = value / (jnp.sqrt(accum_ref[b] + value * value) + 1e-10)
            slot = slot_ref[0, b]
            away = (slot // per) ^ plane_here
            local = slot % per
            held[away, local] = summed
            parts[away, pl.ds(local, 1), :] = jnp.sum(grafted * grafted, axis=0, keepdims=True)
        tail[...] = jnp.zeros_like(tail)
        for k in range(planes):
            for s in range(per):
                out_refs[k][s * rows : (s + 1) * rows, :] = held[k, s]
            for t, term in enumerate(three_terms(parts[k, :per, :])):
                tail[t * per : (t + 1) * per, :] = term
            out_refs[k][per * rows :, :] = tail[...].astype(BF16)

    summed = call(
        sum_body,
        [shape((share_rows, cols), BF16)] * 2
        + [shape((payload_rows, cols), BF16)] * planes,
        [SMEM] + [VMEM] * (reps + 1),
        scratch=[
            pltpu.VMEM((planes, per, rows, cols), BF16),
            pltpu.VMEM((planes, 8, cols), F32),
            pltpu.VMEM((TAIL, cols), F32),
        ],
    )(table, *terms, accum_share)
    shares, payloads = summed[:2], summed[2:]

    arrived = [payloads[0]] + [
        exchange(payloads[k], "fsdp", 2 * k, indices) for k in plane_partners
    ]

    share_firsts = [exchange(shares[m], "rep", ways[m][0], reps) for m in range(2)]
    part_rows = planes * rows + TAIL

    def route_body(slot_ref, *refs):
        in_refs = refs[:planes]
        out_refs = refs[planes : planes + reps]
        parts, tail = refs[planes + reps :]
        rep_here = place()[0]
        total = jnp.zeros((per, cols), F32)
        for ref in in_refs:
            bits = ref[per * rows :, :].astype(F32)
            for t in range(3):
                total = total + bits[t * per : (t + 1) * per]
        parts[:per, :] = total
        tail[...] = jnp.zeros_like(tail)
        for j in range(reps):
            local = slot_ref[0, at_local + (rep_here ^ j)]
            for s in range(per):

                @pl.when(local == s)
                def _():
                    for k in range(planes):
                        out_refs[j][k * rows : (k + 1) * rows, :] = in_refs[k][
                            s * rows : (s + 1) * rows, :
                        ]

            for t, term in enumerate(three_terms(parts[pl.ds(local, 1), :])):
                tail[t : t + 1, :] = term
            out_refs[j][planes * rows :, :] = tail[...].astype(BF16)
    def rest_body(slot_ref, *refs):
        in_refs, whole_ref, rest_refs = refs[:planes], refs[planes + 1], refs[planes + 2 :]
        rep_here = place()[0]
        piece = planes * rows
        for k in range(planes):
            for s in range(per):
                at = s * piece + k * rows
                whole_ref[at : at + rows, :] = in_refs[k][s * rows : (s + 1) * rows, :]
        for j in rep_partners:
            for i in range(per - 1):
                first = (slot_ref[0, at_local + (rep_here ^ j)] + 1 + i) % per * piece
                rest_refs[j - 1][i * piece : (i + 1) * piece, :] = whole_ref[
                    pl.ds(pl.multiple_of(first, piece), piece), :
                ]

    piece_rows = planes * rows
    routed = call(
        route_body,
        [shape((part_rows, cols), BF16)] * reps,
        [SMEM] + [VMEM] * planes,
        scratch=[pltpu.VMEM((8, cols), F32), pltpu.VMEM((TAIL, cols), F32)],
    )(book, *arrived)
    parts = late(routed, *share_firsts, right_other)

    met = [parts[0]] + [exchange(parts[j], "rep", j, reps) for j in rep_partners]
    mine = [jnp.stack(met[i : i + SWAP]) for i in range(0, reps, SWAP)]
    other = [exchange(array, "fsdp", 1, indices) for array in mine]

    whole, *rests = call(
        rest_body,
        [shape((per * piece_rows, cols), BF16)]
        + [shape(((per - 1) * piece_rows, cols), BF16)] * (reps - 1),
        [SMEM] + [VMEM] * planes + [ANY],
    )(book, *arrived, parts[0])
    rests_met = [exchange(rests[j - 1], "rep", j, reps) for j in rep_partners]

    def assemble(grad, rep_here, plane_here, core_here, piece, k, j):
        row = pl.multiple_of((2 * (plane_here ^ k) + core_here) * rows, rows)
        col = pl.multiple_of((rep_here ^ j) * cols, cols)
        grad[pl.ds(row, rows), pl.ds(col, cols)] = piece.astype(scratch_type)

    swaps, side = len(mine), order // 2

    def root_body(slot_ref, *refs):
        mine_refs, other_refs = refs[:swaps], refs[swaps : 2 * swaps]
        left_ref, right_ref, out_ref, graft_ref, grad, matrix, start, sem = refs[2 * swaps :]
        rep_here, plane_here, core_here = place()
        local = slot_ref[0, at_local + rep_here]
        owner, at = local // most, local % most

        @pl.when(owner == core_here)
        def _():
            pltpu.make_async_copy(left_ref.at[at], matrix, sem).start()

        @pl.when(owner != core_here)
        def _():
            pltpu.make_async_copy(right_ref.at[at], matrix, sem).start()

        graft = jnp.zeros((1, cols), F32)
        for j in range(reps):
            for swap_refs, which in ((mine_refs, core_here), (other_refs, 1 - core_here)):
                ref = swap_refs[j // SWAP].at[j % SWAP]
                for k in range(planes):
                    assemble(grad, rep_here, plane_here, which,
                             ref[k * rows : (k + 1) * rows, :], k, j)
                bits = ref[planes * rows :, :].astype(F32)
                graft = graft + jnp.sum(bits[:8], axis=0, keepdims=True)
        line = lax.broadcasted_iota(jnp.int32, graft_ref.shape, 0)
        first = jnp.where(owner == core_here, 1.0, 0.0)
        graft_ref[...] = jnp.where(line == 0, jnp.broadcast_to(graft, graft_ref.shape), first)
        pltpu.make_async_copy(left_ref.at[at], matrix, sem).wait()

        @pl.when(owner == core_here)
        def _():
            value = grad[...].astype(BF16)
            matrix[:side, :] += dot(value[:side], value, 1, 1)
            matrix[side:, side:] += gram(value[side:], 1)
            start[...] = value.astype(F32)

        @pl.when(owner != core_here)
        def _():
            value = grad[...].astype(BF16)
            matrix[:side, :] += dot(value[:, :side], value, 0, 0)
            matrix[side:, side:] += gram(value[:, side:], 0)
            line = lax.broadcasted_iota(jnp.int32, square, 0)
            start[...] = (line == lax.broadcasted_iota(jnp.int32, square, 1)).astype(F32)

        upper, corner = matrix[:side, :], matrix[side:, side:]
        total = jnp.sum(upper[:, :side] * upper[:, :side]) + jnp.sum(corner * corner)
        total = total + 2.0 * jnp.sum(upper[:, side:] * upper[:, side:])
        upper, corner = upper / jnp.sqrt(total), corner / jnp.sqrt(total)
        result = start[...]

        def lower(top, last):
            return jnp.concatenate([top[:, side:].T, last], axis=1)

        for iteration in range(ITERS):
            top = upper.astype(BF16)
            bottom = lower(top, corner.astype(BF16))
            low = jnp.concatenate([top, bottom], axis=0)
            result = 1.25 * result - 0.25 * dot(low, result.astype(BF16))
            if iteration + 1 < ITERS:
                step_top = (dot(top, low) * 0.0625 - 0.625 * upper).astype(BF16)
                step_last = dot(bottom, low[:, side:]) * 0.0625 - 0.625 * corner
                step = jnp.concatenate(
                    [step_top, lower(step_top, step_last.astype(BF16))], axis=0
                )
                twice_top = 1.5625 * upper + dot(top, step)
                twice_last = 1.5625 * corner + dot(bottom, step[:, side:])
                twice_low = twice_top.astype(BF16)
                upper = 1.5625 * twice_top + dot(twice_low, step)
                corner = 1.5625 * twice_last + dot(
                    lower(twice_low, twice_last.astype(BF16)), step[:, side:]
                )
        out_ref[...] = result.astype(BF16)

    root, graft_sum = call(
        root_body,
        [shape(square, BF16), shape((8, cols), F32)],
        [SMEM] + [VMEM] * (2 * swaps) + [ANY, ANY],
        scratch=[
            pltpu.VMEM(square, scratch_type),
            pltpu.VMEM(square, F32),
            pltpu.VMEM(square, F32),
            pltpu.SemaphoreType.DMA,
        ],
        flops=10**9,
        vmem=20,
    )(book, *mine, *other, left_stats, right_other)
    root = fence([root], *rests_met)[0]
    root_other = exchange(root, "fsdp", 1, indices)

    def finish_body(mine_ref, other_ref, graft_ref, *refs):
        out_refs, result = refs[:planes], refs[planes]
        _, plane_here, core_here = place()
        left_here = jnp.sum(graft_ref[1:2, :]) > 0.5

        @pl.when(left_here)
        def _():
            result[...] = dot(mine_ref[...], other_ref[...])

        @pl.when(jnp.logical_not(left_here))
        def _():
            result[...] = dot(other_ref[...], mine_ref[...])

        value = result[...]
        mean = jnp.sum(value * value) / entries
        graft_mean = jnp.sum(graft_ref[0:1, :]) / entries
        scale = jnp.sqrt(graft_mean) / jnp.sqrt(mean + 1e-06)
        for k in range(planes):
            row = pl.multiple_of((2 * (plane_here ^ k) + core_here) * rows, rows)
            out_refs[k][...] = (result[pl.ds(row, rows), :] * scale).astype(BF16)

    slabs = call(
        finish_body,
        [shape((rows, order), BF16)] * planes,
        [VMEM, VMEM, VMEM],
        scratch=[pltpu.VMEM(square, F32)],
        flops=2 * order**3,
    )(root, root_other, graft_sum)

    def side_body(slot_ref, whole_ref, *refs):
        met_refs, rest_refs = refs[: reps - 1], refs[reps - 1 : 2 * reps - 2]
        keep_ref, give_ref, held = refs[2 * reps - 2 :]
        rep_here, _, core_here = place()
        local = slot_ref[0, at_local + rep_here]
        for s in range(per):
            held[0, s] = whole_ref[s * piece_rows : (s + 1) * piece_rows, :]
        for j in rep_partners:
            held[j, local] = met_refs[j - 1][:piece_rows, :]
            for i in range(per - 1):
                held[j, (local + 1 + i) % per] = rest_refs[j - 1][
                    i * piece_rows : (i + 1) * piece_rows, :
                ]
        for j in range(reps):
            for m in range(most):
                keep_ref[j, m] = held[j, core_here * most + m]
                give_ref[j, m] = held[j, (1 - core_here) * most + m]

    held_shape = shape((reps, most, piece_rows, cols), BF16)
    keep, give = call(
        side_body,
        [held_shape, held_shape],
        [SMEM] + [VMEM] * (2 * reps - 1),
        scratch=[pltpu.VMEM((reps, per, piece_rows, cols), BF16)],
    )(book, whole, *met[1:], *rests_met)
    other_side = exchange(give, "fsdp", 1, indices)
    slabs = fence(slabs, other_side)

    returned = [slabs[0]] + [
        exchange(slabs[k], "fsdp", 2 * k, indices) for k in plane_partners
    ]

    share_lasts = [
        exchange(
            fence([jnp.concatenate([shares[m], share_firsts[m]])], slabs[0])[0],
            "rep",
            ways[m][1],
            reps,
        )
        for m in range(2)
    ]

    def stats_body(left_ref, right_ref, after_ref, keep_ref, other_ref,
                   left_out, right_out, token_ref, grad):
        m = pl.program_id(0)
        token_ref[...] = jnp.zeros_like(token_ref)
        rep_here, plane_here, core_here = place()
        for j in range(reps):
            for ref, side in ((keep_ref, core_here), (other_ref, 1 - core_here)):
                for k in range(planes):
                    assemble(grad, rep_here, plane_here, side,
                             ref[j, m, k * rows : (k + 1) * rows, :], k, j)
        value = grad[...].astype(BF16)
        left_out[0] = left_ref[0] + gram(value, 1)
        right_out[0] = right_ref[0] + gram(value, 0)

    token = shape((8, 128), F32)
    slot_block = pl.BlockSpec((1, order, order), lambda m: (m, 0, 0))
    left_new, right_new, stats_token = pl.pallas_call(
        stats_body,
        grid=(most,),
        out_shape=[shape(left_stats.shape, F32), shape(right_stats.shape, F32), token],
        in_specs=[slot_block, slot_block, ANY, VMEM, VMEM],
        out_specs=[slot_block, slot_block, pl.BlockSpec((8, 128), lambda m: (0, 0))],
        scratch_shapes=[pltpu.VMEM(square, scratch_type)],
        compiler_params=pltpu.CompilerParams(vmem_limit_bytes=20 * MIB),
        cost_estimate=pl.CostEstimate(
            flops=1, bytes_accessed=1, transcendentals=0
        ),
    )(left_stats, right_stats, slabs[0], keep, other_side)

    def pick_body(slot_ref, *refs):
        out_ref = refs[-1]
        for k in range(planes):
            spot = slot_ref[0, at_place + k]

            @pl.when(spot >= 0)
            def _():
                out_ref[spot] = refs[k][...]

    picked = call(
        pick_body,
        shape((share, rows, order), BF16),
        [SMEM] + [VMEM] * planes + [ANY],
    )(book, *returned, stats_token)
    picked = fence([picked], flops=10**8)[0]
    gathered = [picked] + [exchange(picked, "rep", j, reps) for j in rep_partners]

    def accum_body(accum_ref, vocab_ref, after_ref, *refs):

        def piece(j, first, count):
            m, at = first // share_rows, first % share_rows
            near, far = ways[m]
            ref, base = {
                0: (refs[m], 0),
                near: (refs[2 + m], 0),
                far: (refs[4 + m], 0),
                near ^ far: (refs[4 + m], share_rows),
            }[j]
            return ref[base + at : base + at + count, :].astype(F32)

        accum_out, vocab_out, step_out, token_ref = refs[6:]
        token_ref[...] = jnp.zeros_like(token_ref)
        rep_here = place()[0]
        for j in range(reps):
            at = pl.ds(pl.multiple_of((rep_here ^ j) * cols, cols), cols)
            for b in range(blocks):
                value = piece(j, b * rows, rows)
                accum_out[b, :, at] = accum_ref[b, :, at] + value * value
            for i in range(chunks):
                value = piece(j, grad_rows + i * pair_rows, pair_rows)
                value = value.reshape(vocab_own.shape[:2] + (cols,))
                start = pl.multiple_of((rep_here ^ j) * vocab_cols + i * cols, cols)
                at_vocab = pl.ds(start, cols)
                accum = vocab_ref[:, :, at_vocab] + value * value
                vocab_out[:, :, at_vocab] = accum
                step_out[:, :, at_vocab] = (value / (jnp.sqrt(accum) + 1e-10)).astype(BF16)

    graft_accum_new, vocab_accum_new, vocab_step, accum_token = call(
        accum_body,
        [
            shape(graft_accum.shape, F32),
            shape(vocab_accum.shape, F32),
            shape(vocab_accum.shape, BF16),
            token,
        ],
        [VMEM, VMEM, ANY] + [VMEM] * 6,
        vmem=12,
    )(graft_accum, vocab_accum, picked, *shares, *share_firsts, *share_lasts)

    def place_body(slot_ref, *refs):
        out_ref, sem = refs[reps + 1 :]
        rep_here = place()[0]

        copies = []
        for j in range(reps):
            for m in range(share):
                block = slot_ref[0, at_block + m * reps + (rep_here ^ j)]
                copies.append(
                    pltpu.make_async_copy(
                        refs[j].at[m], out_ref.at[block], sem.at[j * share + m]
                    )
                )
                copies[-1].start()
        for copy in copies:
            copy.wait()

    direction = call(
        place_body,
        shape((blocks, rows, order), BF16),
        [SMEM] + [VMEM] * reps + [ANY],
        out_specs=HBM,
        scratch=[pltpu.SemaphoreType.DMA((blocks,))],
    )(book, *gathered, accum_token)
    return (direction, graft_accum_new, left_new, right_new, vocab_accum_new, vocab_step)


def solution(mesh):
    in_specs = (
        P("rep", None, "fsdp", None),
        P(None, "fsdp", None),
        P("fsdp", None, None),
        P("fsdp", None, None),
        P(),
        P("rep", None, "fsdp", None),
        P(None, "fsdp", None),
    )
    out_specs = (
        P(None, "fsdp", None),
        P(None, "fsdp", None),
        P("fsdp", None, None),
        P("fsdp", None, None),
        P(None, "fsdp", None),
        P(None, "fsdp", None),
    )
    return jax.shard_map(
        on_device, mesh=mesh, in_specs=in_specs, out_specs=out_specs, check_vma=False
    )
```
